768 devices in a mesh: blk: 12 (over x, z_hi), col: 64 (over z_lo, y, core).
Axes of the slice: x: 4, y: 8, z: 12 (z_hi: 3, z_lo: 4; z = z_hi * 4 + z_lo), core: 2. Of those that a mesh axis runs over, the one named last changes fastest.
Arguments:
- vectors: float32 [49152, 64], P(('blk', 'col')), may hold values from -6 to 6
- blocks: bfloat16 [12, 64, 4, 2, 256, 256], P('blk', 'col'), may hold values from -0.046875 to 0.046875
- row_blocks: int32 [12, 64, 4, 2], P('blk', 'col'), may hold values from 0 to 15, as said below
- col_blocks: int32 [12, 64, 4, 2], P('blk', 'col'), may hold values from 0 to 15, as said below
Outputs:
- product: float32 [49152, 64], P(('blk', 'col'))
The draws below stay inside these ranges and needn't reach their ends.
Inputs may be any that keep to these rules, and one draw needn't show every extreme that they name: Within one shard and distance no pair of row_blocks and col_blocks occurs twice; at distance 0 the row block is at most the column block. `col_blocks`: drawn together with row_blocks, as stated there.
All inputs are finite; a program needn't handle non-finite values.
Results may differ from the reference program's by a relative error of at most 0.0029.
Values may be sent and summed in bfloat16 or wider, within the bound.
No kernel may reach another device: no remote copies, remote signals or barrier semaphores. Data moves between devices by JAX's collectives and lax.ppermute only.
A program may use at most 32 MiB of HBM per device.

```python
import jax
import jax.numpy as jnp

BS = 256
NV = 64
NBB = 16
SLOTS = 2
STEPS = 4
NROWS = 49152
N_BLK = 12
N_COL = 64


def pick_positions(key):
    total = NBB * NBB
    grid = jnp.arange(total, dtype=jnp.int32)
    lower = grid // NBB > grid % NBB

    def one_pair(shard, step):
        inner = jax.random.fold_in(jax.random.fold_in(jax.random.fold_in(key, 7), shard), step)
        ranks = jax.random.permutation(inner, total).astype(jnp.int32)
        score = jnp.where(jnp.logical_and(step == 0, lower), ranks + total, ranks)
        chosen = jnp.argsort(score, stable=True)[:N_COL * SLOTS]
        return chosen.astype(jnp.int32)
    shard_ids = jnp.arange(N_BLK, dtype=jnp.int32)
    step_ids = jnp.arange(STEPS, dtype=jnp.int32)
    table = jax.vmap(lambda shard: jax.vmap(lambda step: one_pair(shard, step))(step_ids))(shard_ids)
    table = table.reshape(N_BLK, STEPS, N_COL, SLOTS).transpose(0, 2, 1, 3)
    return table


def draw_row_blocks(key, part):
    return (pick_positions(key) // NBB).astype(jnp.int32)


def draw_col_blocks(key, part):
    return (pick_positions(key) % NBB).astype(jnp.int32)


def level_of(stream_key, dims, split, low, top_value):
    def one(position, shards_of):
        draws = jax.random.uniform(jax.random.fold_in(jax.random.fold_in(stream_key, 6), position), (shards_of,), jnp.float32, low / len(split), top_value / len(split))
        return jnp.repeat(jnp.exp(draws), dims[position] // shards_of).reshape((-1,) + (1,) * (len(dims) - position - 1))

    gain = one(*split[0])
    for cut in split[1:]:
        gain = gain * one(*cut)
    return gain


def bell_draw(stream_key, shape, deviation, bound, cuts=(), held_as=jnp.bfloat16):
    values = deviation * jax.random.normal(stream_key, shape, jnp.float32)
    if cuts:
        values = values * level_of(stream_key, shape, cuts, -0.22, 0.18)
    return jnp.clip(values, -bound, bound).astype(held_as)


def setup_inputs(seed: int = 0) -> dict:
    keys = jax.random.split(jax.random.key(seed), 5)
    return {
        "vectors": bell_draw(keys[0], (NROWS, NV), 1.0, 6.0, ((0, 768),), jnp.float32),
        "blocks": bell_draw(keys[1], (N_BLK, N_COL, STEPS, SLOTS, BS, BS), (2 * STEPS * N_COL * SLOTS * BS // NBB) ** -0.5, 0.046875, ((0, 12), (1, 64))),
        "row_blocks": draw_row_blocks(jax.random.fold_in(keys[4], 71), 0),
        "col_blocks": draw_col_blocks(jax.random.fold_in(keys[4], 71), 0),
    }


def reference(vectors, blocks, row_blocks, col_blocks):
    shards = vectors.astype(jnp.bfloat16).reshape(N_BLK, NBB, BS, NV)
    result = jnp.zeros((N_BLK, NBB, BS, NV), jnp.float32)
    for shard in range(N_BLK):
        for step in range(STEPS):
            source = (shard - step) % N_BLK
            stored = blocks[shard, :, step].reshape(N_COL * SLOTS, BS, BS).astype(jnp.float32)
            rows_at = row_blocks[shard, :, step].reshape(N_COL * SLOTS).astype(jnp.int32)
            cols_at = col_blocks[shard, :, step].reshape(N_COL * SLOTS).astype(jnp.int32)
            right = shards[source][cols_at].astype(jnp.float32)
            left = shards[shard][rows_at].astype(jnp.float32)
            direct = jnp.einsum("kij,kjv->kiv", stored, right)
            transposed = jnp.einsum("kji,kjv->kiv", stored, left)
            result = result.at[shard, rows_at].add(direct)
            result = result.at[source, cols_at].add(transposed)
    return result.reshape(NROWS, NV)
```

```python
import jax
import jax.numpy as jnp
from jax import lax
from jax.experimental import pallas as pl
from jax.experimental.pallas import tpu as pltpu
from jax.sharding import PartitionSpec as P

BF16 = jnp.bfloat16
F32 = jnp.float32
COL = 64
NBB = 16
NV = 64
BS = 256
STEPS = 4
SLOTS = 2
HALF = 128
CHUNK = 32
MIX = 16
REMOTE = (STEPS - 1) * SLOTS


def passed_along(block, axis, distance):
    n = lax.axis_size(axis)
    return lax.ppermute(block, axis, [((i - distance) % n, i) for i in range(n)])


def exchanged(flat, rows):
    pieces = lax.all_to_all(flat.reshape(COL, rows, HALF), "col", 0, 0, tiled=True)
    return pieces.reshape(COL * rows, HALF)


def dense_block(held, index):
    tops, bottoms = [], []
    for quarter in range(4):
        start = pl.multiple_of((index * 4 + quarter) * CHUNK, CHUNK)
        piece = held[pl.ds(start, CHUNK), :]
        tops.append(piece[:, :64])
        bottoms.append(piece[:, 64:])
    top = jnp.concatenate(tops, axis=1)
    bottom = jnp.concatenate(bottoms, axis=1)
    return jnp.concatenate([top, bottom], axis=0)


def times(left, block):
    return lax.dot_general(left, block, (((1,), (0,)), ((), ())), preferred_element_type=F32)


def times_transposed(left, block):
    return lax.dot_general(left, block, (((1,), (1,)), ((), ())), preferred_element_type=F32)


def every(row, stride=MIX, count=COL):
    return pl.ds(row, count, stride=stride)


def remote_products(rows_at, cols_at, held, blocks, h1, h2, h3, out, work):
    for step in range(1, STEPS):
        for k in range(SLOTS):
            slot = (step - 1) * SLOTS + k
            left = dense_block(held, rows_at[step, k])
            partial = times(left, blocks[step * SLOTS + k])
            work[every(2 * slot), :] = partial[:, :HALF]
            work[every(2 * slot + 1), :] = partial[:, HALF:]
    work[every(12), :] = jnp.concatenate([h1[...], h2[...]], axis=1).astype(F32)
    lane = lax.broadcasted_iota(jnp.int32, (COL, 64), 1)
    listed = jnp.zeros((COL, 64), jnp.int32)
    for step in range(STEPS):
        for k in range(SLOTS):
            at = step * SLOTS + k
            listed = jnp.where(lane == at, cols_at[step, k], listed)
    work[every(13), :] = jnp.concatenate([h3[...].astype(F32), listed.astype(F32)], axis=1)
    work[every(14), :] = jnp.zeros((COL, HALF), F32)
    work[every(15), :] = jnp.zeros((COL, HALF), F32)
    out[...] = work[...].astype(BF16)


def owners_turn(arrived, out, came, work):
    came[...] = arrived[...].astype(F32)
    asked = came[every(13), :]
    asked_t = jnp.transpose(asked)
    block_down = lax.broadcasted_iota(jnp.int32, (NBB, COL), 0).astype(F32)
    block_along = lax.broadcasted_iota(jnp.int32, (COL, NBB), 1).astype(F32)
    quarters_a = [came[pl.ds(12 + MIX * q, NBB, stride=4 * MIX), :] for q in range(4)]
    quarters_b = [came[pl.ds(13 + MIX * q, NBB, stride=4 * MIX), :] for q in range(4)]
    columns = [
        jnp.concatenate([q[:, :64] for q in quarters_a], axis=1),
        jnp.concatenate([q[:, 64:] for q in quarters_a], axis=1),
        jnp.concatenate([q[:, :64] for q in quarters_b], axis=1),
    ]
    sums = []
    for step in range(1, STEPS):
        total = None
        own = columns[step - 1].astype(BF16)
        for k in range(SLOTS):
            slot = (step - 1) * SLOTS + k
            lane = 64 + step * SLOTS + k
            partial = jnp.concatenate([came[every(2 * slot), :], came[every(2 * slot + 1), :]], axis=1)
            goes_to = (asked_t[lane : lane + 1, :] == block_down).astype(F32).astype(BF16)
            part = times(goes_to, partial.astype(BF16))
            total = part if total is None else total + part
            wants = (asked[:, lane : lane + 1] == block_along).astype(F32).astype(BF16)
            answer = times(wants, own)
            work[every(2 * slot), :] = answer[:, :HALF]
            work[every(2 * slot + 1), :] = answer[:, HALF:]
        sums.append(total)
    highs = [s.astype(BF16).astype(F32) for s in sums]
    lows = [s - h for s, h in zip(sums, highs)]
    for q in range(4):
        part = slice(64 * q, 64 * q + 64)
        for row, (s1, s2, s3) in ((12, highs), (14, lows)):
            work[pl.ds(row + MIX * q, NBB, stride=4 * MIX), :] = jnp.concatenate(
                [s1[:, part], s2[:, part]], axis=1
            )
            work[pl.ds(row + 1 + MIX * q, NBB, stride=4 * MIX), :] = jnp.concatenate(
                [s3[:, part], jnp.zeros((NBB, 64), F32)], axis=1
            )
    out[...] = work[...].astype(BF16)


def own_products(rows_at, cols_at, held, blocks, arrived, out, u1, u2, u3, came, total):
    came[...] = arrived[...].astype(F32)
    pair = came[every(12), :] + came[every(14), :]
    third = came[every(13), :] + came[every(15), :]
    u1[...] = pair[:, :64]
    u2[...] = pair[:, 64:]
    u3[...] = third[:, :64]
    total[...] = jnp.zeros_like(total)
    for k in range(SLOTS):
        row, col = rows_at[0, k], cols_at[0, k]
        total[row] += times_transposed(dense_block(held, col), blocks[k])
        total[col] += times(dense_block(held, row), blocks[k])
    for step in range(1, STEPS):
        for k in range(SLOTS):
            slot = (step - 1) * SLOTS + k
            right = jnp.concatenate([came[every(2 * slot), :], came[every(2 * slot + 1), :]], axis=1)
            total[rows_at[step, k]] += times_transposed(right.astype(BF16), blocks[step * SLOTS + k])
    for row in range(NBB):
        whole = total[row]
        for q in range(4):
            part = whole[:, 64 * q : 64 * q + 64]
            start = (row * 4 + q) * CHUNK
            out[start : start + CHUNK, :] = jnp.concatenate([part[:32], part[32:]], axis=1).astype(BF16)


def gathered_sum(arrived, r1, r2, r3, out):
    sums = [arrived[i * CHUNK : (i + 1) * CHUNK, :].astype(F32) for i in range(4)]
    for i in range(4, COL):
        sums[i % 4] += arrived[i * CHUNK : (i + 1) * CHUNK, :].astype(F32)
    packed = (sums[0] + sums[1]) + (sums[2] + sums[3])
    own = jnp.concatenate([packed[:, :64], packed[:, 64:]], axis=0)
    total = own + ((r1[...] + r2[...]) + r3[...])
    out[...] = jnp.transpose(jnp.concatenate([total, total], axis=1))[:64]


VM = pl.BlockSpec(memory_space=pltpu.VMEM)
SM = pl.BlockSpec(memory_space=pltpu.SMEM)
PARAMS = pltpu.CompilerParams(vmem_limit_bytes=24 * 1024 * 1024)


def shape_of(shape, dtype):
    return jax.ShapeDtypeStruct(shape, dtype)


def per_device(vectors, blocks, row_blocks, col_blocks):
    stored = blocks.reshape(STEPS * SLOTS, BS, BS)
    rows_at = row_blocks[0, 0]
    cols_at = col_blocks[0, 0]
    turned = vectors.T.astype(BF16)
    near = [passed_along(turned, "blk", step) for step in range(1, STEPS)]
    packed = jnp.concatenate([turned[:32], turned[32:]], axis=1)
    held = exchanged(jnp.broadcast_to(packed[None], (COL, CHUNK, HALF)), CHUNK)
    sent = pl.pallas_call(
        remote_products,
        out_shape=shape_of((COL * MIX, HALF), BF16),
        in_specs=[SM, SM, VM, VM, VM, VM, VM],
        out_specs=VM,
        scratch_shapes=[pltpu.VMEM((COL * MIX, HALF), F32)],
        compiler_params=PARAMS,
    )(rows_at, cols_at, held, stored, *near)
    arrived = exchanged(sent, MIX)
    answers = pl.pallas_call(
        owners_turn,
        out_shape=shape_of((COL * MIX, HALF), BF16),
        in_specs=[VM],
        out_specs=VM,
        scratch_shapes=[pltpu.VMEM((COL * MIX, HALF), F32), pltpu.VMEM((COL * MIX, HALF), F32)],
        compiler_params=PARAMS,
    )(arrived)
    answered = exchanged(answers, MIX)
    piece = shape_of((NV, 64), F32)
    partials, u1, u2, u3 = pl.pallas_call(
        own_products,
        out_shape=(shape_of((COL * CHUNK, HALF), BF16), piece, piece, piece),
        in_specs=[SM, SM, VM, VM, VM],
        out_specs=(VM, VM, VM, VM),
        scratch_shapes=[pltpu.VMEM((COL * MIX, HALF), F32), pltpu.VMEM((NBB, NV, BS), F32)],
        compiler_params=PARAMS,
    )(rows_at, cols_at, held, stored, answered)
    home = [passed_along(u, "blk", -step) for step, u in ((1, u1), (2, u2), (3, u3))]
    collected = exchanged(partials, CHUNK)
    return pl.pallas_call(
        gathered_sum,
        out_shape=shape_of((64, NV), F32),
        in_specs=[VM, VM, VM, VM],
        out_specs=VM,
        compiler_params=PARAMS,
    )(collected, *home)


def solution(mesh):
    return jax.shard_map(
        per_device,
        mesh=mesh,
        in_specs=(
            P(("blk", "col"), None),
            P("blk", "col", None, None, None, None),
            P("blk", "col", None, None),
            P("blk", "col", None, None),
        ),
        out_specs=P(("blk", "col"), None),
        check_vma=False,
    )
```

```python
import jax
import jax.numpy as jnp
from jax import lax
from jax.experimental import pallas as pl
from jax.experimental.pallas import tpu as pltpu
from jax.sharding import PartitionSpec as P

BF16 = jnp.bfloat16
F32 = jnp.float32
COL = 64
NBB = 16
NV = 64
BS = 256
STEPS = 4
SLOTS = 2
HALF = 128
CHUNK = 32


def passed_along(block, axis, distance):
    n = lax.axis_size(axis)
    return lax.ppermute(block, axis, [((i - distance) % n, i) for i in range(n)])


def exchanged(flat, rows):
    pieces = lax.all_to_all(flat.reshape(COL, rows, HALF), "col", 0, 0, tiled=True)
    return pieces.reshape(COL * rows, HALF)


def dense_block(held, index):
    tops, bottoms = [], []
    for quarter in range(4):
        start = pl.multiple_of((index * 4 + quarter) * CHUNK, CHUNK)
        piece = held[pl.ds(start, CHUNK), :]
        tops.append(piece[:, :64])
        bottoms.append(piece[:, 64:])
    top = jnp.concatenate(tops, axis=1)
    bottom = jnp.concatenate(bottoms, axis=1)
    return jnp.concatenate([top, bottom], axis=0)


def times(left, block):
    return lax.dot_general(left, block, (((1,), (0,)), ((), ())), preferred_element_type=F32)


def times_transposed(left, block):
    return lax.dot_general(left, block, (((1,), (1,)), ((), ())), preferred_element_type=F32)


def neighbours_blocks(rows_at, cols_at, far1, far2, far3, held, blocks, *outs):
    picked, partials = outs[:3], outs[3:]
    for step, far in ((1, far1), (2, far2), (3, far3)):
        for k in range(SLOTS):
            picked[step - 1][NV * k : NV * (k + 1), :] = dense_block(held, far[step, k])
    for step in range(1, STEPS):
        for k in range(SLOTS):
            left = dense_block(held, rows_at[step, k])
            partial = times(left, blocks[step * SLOTS + k])
            partials[step - 1][NV * k : NV * (k + 1), :] = partial.astype(BF16)


def own_products(rows_at, cols_at, far1, far2, far3, held, blocks, g1, g2, g3, p1, p2, p3, out, total):
    total[...] = jnp.zeros_like(total)
    for k in range(SLOTS):
        row, col = rows_at[0, k], cols_at[0, k]
        total[row] += times_transposed(dense_block(held, col), blocks[k])
        total[col] += times(dense_block(held, row), blocks[k])
    for step, right, back, far in ((1, g1, p1, far1), (2, g2, p2, far2), (3, g3, p3, far3)):
        for k in range(SLOTS):
            part = slice(NV * k, NV * (k + 1))
            total[rows_at[step, k]] += times_transposed(right[part, :], blocks[step * SLOTS + k])
            total[far[step, k]] += back[part, :].astype(F32)
    for row in range(NBB):
        whole = total[row]
        for q in range(4):
            part = whole[:, 64 * q : 64 * q + 64]
            start = (row * 4 + q) * CHUNK
            out[start : start + CHUNK, :] = jnp.concatenate([part[:32], part[32:]], axis=1).astype(BF16)


def gathered_sum(arrived, out):
    sums = [arrived[i * CHUNK : (i + 1) * CHUNK, :].astype(F32) for i in range(4)]
    for i in range(4, COL):
        sums[i % 4] += arrived[i * CHUNK : (i + 1) * CHUNK, :].astype(F32)
    packed = (sums[0] + sums[1]) + (sums[2] + sums[3])
    own = jnp.concatenate([packed[:, :64], packed[:, 64:]], axis=0)
    out[...] = jnp.transpose(jnp.concatenate([own, own], axis=1))[:64]


VM = pl.BlockSpec(memory_space=pltpu.VMEM)
SM = pl.BlockSpec(memory_space=pltpu.SMEM)
PARAMS = pltpu.CompilerParams(vmem_limit_bytes=24 * 1024 * 1024)


def shape_of(shape, dtype):
    return jax.ShapeDtypeStruct(shape, dtype)


def per_device(vectors, blocks, row_blocks, col_blocks):
    stored = blocks.reshape(STEPS * SLOTS, BS, BS)
    rows_at = row_blocks[0, 0]
    cols_at = col_blocks[0, 0]
    turned = vectors.T.astype(BF16)
    far = [passed_along(cols_at, "blk", -step) for step in range(1, STEPS)]
    packed = jnp.concatenate([turned[:32], turned[32:]], axis=1)
    held = exchanged(jnp.broadcast_to(packed[None], (COL, CHUNK, HALF)), CHUNK)
    pair = shape_of((SLOTS * NV, BS), BF16)
    sent = pl.pallas_call(
        neighbours_blocks,
        out_shape=(pair,) * 6,
        in_specs=[SM] * 5 + [VM] * 2,
        out_specs=(VM,) * 6,
        compiler_params=PARAMS,
    )(rows_at, cols_at, *far, held, stored)
    right = [passed_along(sent[step - 1], "blk", step) for step in range(1, STEPS)]
    back = [passed_along(sent[step + 2], "blk", -step) for step in range(1, STEPS)]
    sums = pl.pallas_call(
        own_products,
        out_shape=shape_of((COL * CHUNK, HALF), BF16),
        in_specs=[SM] * 5 + [VM] * 8,
        out_specs=VM,
        scratch_shapes=[pltpu.VMEM((NBB, NV, BS), F32)],
        compiler_params=PARAMS,
    )(rows_at, cols_at, *far, held, stored, *right, *back)
    return pl.pallas_call(
        gathered_sum,
        out_shape=shape_of((64, NV), F32),
        in_specs=[VM],
        out_specs=VM,
        compiler_params=PARAMS,
    )(exchanged(sums, CHUNK))


def solution(mesh):
    return jax.shard_map(
        per_device,
        mesh=mesh,
        in_specs=(
            P(("blk", "col"), None),
            P("blk", "col", None, None, None, None),
            P("blk", "col", None, None),
            P("blk", "col", None, None),
        ),
        out_specs=P(("blk", "col"), None),
        check_vma=False,
    )
```

```python
import jax
import jax.numpy as jnp
from jax import lax
from jax.experimental import pallas as pl
from jax.experimental.pallas import tpu as pltpu
from jax.sharding import Mesh, PartitionSpec as P

BF16 = jnp.bfloat16
F32 = jnp.float32
COL = 64
NBB = 16
NV = 64
BS = 256
STEPS = 4
AXES = ("blk", "pos", "core")
SLOTS = 2
HALF = 128
CHUNK = 32


def routed(block, near, far):
    sizes = [lax.axis_size(axis) for axis in AXES]
    n, positions, cores = sizes
    route = []
    for shard in range(n):
        for place in range(positions * cores):
            step = far if place % cores else near
            route.append((shard * positions * cores + place, (shard + step) % n * positions * cores + place))
    return lax.ppermute(block, AXES, route)


def exchanged(flat, rows):
    pieces = lax.all_to_all(flat.reshape(COL, rows, HALF), ("pos", "core"), 0, 0, tiled=True)
    return pieces.reshape(COL * rows, HALF)


def swapped(pair):
    return lax.all_to_all(pair, "core", 0, 0, tiled=True)


def dense_block(held, index):
    tops, bottoms = [], []
    for quarter in range(4):
        start = pl.multiple_of((index * 4 + quarter) * CHUNK, CHUNK)
        piece = held[pl.ds(start, CHUNK), :]
        tops.append(piece[:, :64])
        bottoms.append(piece[:, 64:])
    top = jnp.concatenate(tops, axis=1)
    bottom = jnp.concatenate(bottoms, axis=1)
    return jnp.concatenate([top, bottom], axis=0)


def times(left, block):
    return lax.dot_general(left, block, (((1,), (0,)), ((), ())), preferred_element_type=F32)


def times_transposed(left, block):
    return lax.dot_general(left, block, (((1,), (1,)), ((), ())), preferred_element_type=F32)


def neighbours_blocks(rows_at, far, far3, held, blocks, picked, picked3, partials, partials3):
    mine = 1 + lax.axis_index("core")
    for k in range(SLOTS):
        part = slice(NV * k, NV * (k + 1))
        for core in range(2):
            picked[core, part, :] = dense_block(held, far[core, mine, k])
        picked3[part, :] = dense_block(held, far3[3, k])
    for step in range(1, STEPS):
        for k in range(SLOTS):
            part = slice(NV * k, NV * (k + 1))
            left = dense_block(held, rows_at[step, k])
            partial = times(left, blocks[step * SLOTS + k]).astype(BF16)
            if step < 3:
                partials[step - 1, part, :] = partial
            else:
                partials3[part, :] = partial


def own_products(rows_at, cols_at, far, far3, held, blocks, right, right3, back, back3, out, total):
    mine = 1 + lax.axis_index("core")
    total[...] = jnp.zeros_like(total)
    for k in range(SLOTS):
        part = slice(NV * k, NV * (k + 1))
        row, col = rows_at[0, k], cols_at[0, k]
        total[row] += times_transposed(dense_block(held, col), blocks[k])
        total[col] += times(dense_block(held, row), blocks[k])
        for step in range(1, STEPS):
            came = right[step - 1, part, :] if step < 3 else right3[part, :]
            total[rows_at[step, k]] += times_transposed(came, blocks[step * SLOTS + k])
        for core in range(2):
            total[far[core, mine, k]] += back[core, part, :].astype(F32)
        total[far3[3, k]] += back3[part, :].astype(F32)
    for row in range(NBB):
        whole = total[row]
        for q in range(4):
            part = whole[:, 64 * q : 64 * q + 64]
            start = (row * 4 + q) * CHUNK
            out[start : start + CHUNK, :] = jnp.concatenate([part[:32], part[32:]], axis=1).astype(BF16)


def gathered_sum(arrived, out):
    sums = [arrived[i * CHUNK : (i + 1) * CHUNK, :].astype(F32) for i in range(4)]
    for i in range(4, COL):
        sums[i % 4] += arrived[i * CHUNK : (i + 1) * CHUNK, :].astype(F32)
    packed = (sums[0] + sums[1]) + (sums[2] + sums[3])
    own = jnp.concatenate([packed[:, :64], packed[:, 64:]], axis=0)
    out[...] = jnp.transpose(jnp.concatenate([own, own], axis=1))[:64]


VM = pl.BlockSpec(memory_space=pltpu.VMEM)
SM = pl.BlockSpec(memory_space=pltpu.SMEM)
PARAMS = pltpu.CompilerParams(vmem_limit_bytes=24 * 1024 * 1024)


def shape_of(shape, dtype):
    return jax.ShapeDtypeStruct(shape, dtype)


def per_device(vectors, blocks, row_blocks, col_blocks):
    stored = blocks.reshape(STEPS * SLOTS, BS, BS)
    rows_at = row_blocks[0, 0]
    cols_at = col_blocks[0, 0]
    turned = vectors.T.astype(BF16)
    far = routed(lax.all_gather(cols_at, "core"), -1, -2)
    far3 = routed(cols_at, -3, -3)
    packed = jnp.concatenate([turned[:32], turned[32:]], axis=1)
    held = exchanged(jnp.broadcast_to(packed[None], (COL, CHUNK, HALF)), CHUNK)
    one = shape_of((SLOTS * NV, BS), BF16)
    two = shape_of((2, SLOTS * NV, BS), BF16)
    picked, picked3, partials, partials3 = pl.pallas_call(
        neighbours_blocks,
        out_shape=(two, one, two, one),
        in_specs=[SM] * 3 + [VM] * 2,
        out_specs=(VM,) * 4,
        compiler_params=PARAMS,
    )(rows_at, far, far3, held, stored)
    right = swapped(routed(picked, 1, 2))
    right3 = routed(picked3, 3, 3)
    back = routed(swapped(partials), -1, -2)
    back3 = routed(partials3, -3, -3)
    sums = pl.pallas_call(
        own_products,
        out_shape=shape_of((COL * CHUNK, HALF), BF16),
        in_specs=[SM] * 4 + [VM] * 6,
        out_specs=VM,
        scratch_shapes=[pltpu.VMEM((NBB, NV, BS), F32)],
        compiler_params=PARAMS,
    )(rows_at, cols_at, far, far3, held, stored, right, right3, back, back3)
    return pl.pallas_call(
        gathered_sum,
        out_shape=shape_of((64, NV), F32),
        in_specs=[VM],
        out_specs=VM,
        compiler_params=PARAMS,
    )(exchanged(sums, CHUNK))


def solution(mesh):
    shards, places = mesh.devices.shape
    fine = Mesh(mesh.devices.reshape(shards, places // 2, 2), AXES)
    rest = ("pos", "core")
    return jax.shard_map(
        per_device,
        mesh=fine,
        in_specs=(
            P(AXES, None),
            P("blk", rest, None, None, None, None),
            P("blk", rest, None, None),
            P("blk", rest, None, None),
        ),
        out_specs=P(AXES, None),
        check_vma=False,
    )
```

```python
import jax
import jax.numpy as jnp
from jax import lax
from jax.experimental import pallas as pl
from jax.experimental.pallas import tpu as pltpu
from jax.sharding import Mesh, PartitionSpec as P

BF16 = jnp.bfloat16
F32 = jnp.float32
COL = 64
NBB = 16
NV = 64
BS = 256
STEPS = 4
AXES = ("blk", "pos", "core")
SLOTS = 2
HALF = 128
CHUNK = 32


def routed(block, near, far):
    sizes = [lax.axis_size(axis) for axis in AXES]
    n, positions, cores = sizes
    route = []
    for shard in range(n):
        for place in range(positions * cores):
            step = far if place % cores else near
            route.append((shard * positions * cores + place, (shard + step) % n * positions * cores + place))
    return lax.ppermute(block, AXES, route)


def exchanged(flat, rows):
    pieces = lax.all_to_all(flat.reshape(COL, rows, HALF), ("pos", "core"), 0, 0, tiled=True)
    return pieces.reshape(COL * rows, HALF)


def dense_block(held, index):
    tops, bottoms = [], []
    for quarter in range(4):
        start = pl.multiple_of((index * 4 + quarter) * CHUNK, CHUNK)
        piece = held[pl.ds(start, CHUNK), :]
        tops.append(piece[:, :64])
        bottoms.append(piece[:, 64:])
    top = jnp.concatenate(tops, axis=1)
    bottom = jnp.concatenate(bottoms, axis=1)
    return jnp.concatenate([top, bottom], axis=0)


def times(left, block):
    return lax.dot_general(left, block, (((1,), (0,)), ((), ())), preferred_element_type=F32)


def times_transposed(left, block):
    return lax.dot_general(left, block, (((1,), (1,)), ((), ())), preferred_element_type=F32)


def prepared(vectors, out):
    rows = vectors[...]
    turned = jnp.transpose(jnp.concatenate([rows, rows], axis=1))
    packed = jnp.concatenate([turned[:32], turned[32:64]], axis=1).astype(BF16)
    for i in range(COL):
        out[i * CHUNK : (i + 1) * CHUNK, :] = packed


def shared_block(blocks, other, me, core, k):
    if core == 0:
        return blocks[(1 + me) * SLOTS + k]
    return other[k]


def transposed_products(lists, held, blocks, other, partials, partials3):
    me = lax.axis_index("core")
    for k in range(SLOTS):
        part = slice(NV * k, NV * (k + 1))
        for core, owner in enumerate((me, 1 - me)):
            left = dense_block(held, lists[owner, 0, 1 + me, k])
            partials[core, part, :] = times(left, shared_block(blocks, other, me, core, k)).astype(BF16)
        left = dense_block(held, lists[me, 0, 3, k])
        partials3[part, :] = times(left, blocks[3 * SLOTS + k]).astype(BF16)


def asked_blocks(far, far3, held, picked, picked3):
    me = lax.axis_index("core")
    for k in range(SLOTS):
        part = slice(NV * k, NV * (k + 1))
        for core, owner in enumerate((me, 1 - me)):
            picked[core, part, :] = dense_block(held, far[owner, 1, 1 + me, k])
        picked3[part, :] = dense_block(held, far3[me, 1, 3, k])


def own_products(lists, far, far3, held, blocks, other, right, right3, back, back3, out, total):
    me = lax.axis_index("core")
    total[...] = jnp.zeros_like(total)
    for k in range(SLOTS):
        part = slice(NV * k, NV * (k + 1))
        row, col = lists[me, 0, 0, k], lists[me, 1, 0, k]
        total[row] += times_transposed(dense_block(held, col), blocks[k])
        total[col] += times(dense_block(held, row), blocks[k])
        for core, owner in enumerate((me, 1 - me)):
            block = shared_block(blocks, other, me, core, k)
            total[lists[owner, 0, 1 + me, k]] += times_transposed(right[core, part, :], block)
            total[far[owner, 1, 1 + me, k]] += back[core, part, :].astype(F32)
        total[lists[me, 0, 3, k]] += times_transposed(right3[part, :], blocks[3 * SLOTS + k])
        total[far3[me, 1, 3, k]] += back3[part, :].astype(F32)
    for row in range(NBB):
        whole = total[row]
        for q in range(4):
            part = whole[:, 64 * q : 64 * q + 64]
            start = (row * 4 + q) * CHUNK
            out[start : start + CHUNK, :] = jnp.concatenate([part[:32], part[32:]], axis=1).astype(BF16)


def gathered_sum(arrived, out):
    sums = [arrived[i * CHUNK : (i + 1) * CHUNK, :].astype(F32) for i in range(4)]
    for i in range(4, COL):
        sums[i % 4] += arrived[i * CHUNK : (i + 1) * CHUNK, :].astype(F32)
    packed = (sums[0] + sums[1]) + (sums[2] + sums[3])
    own = jnp.concatenate([packed[:, :64], packed[:, 64:]], axis=0)
    out[...] = jnp.transpose(jnp.concatenate([own, own], axis=1))[:64]


VM = pl.BlockSpec(memory_space=pltpu.VMEM)
SM = pl.BlockSpec(memory_space=pltpu.SMEM)
PARAMS = pltpu.CompilerParams(vmem_limit_bytes=24 * 1024 * 1024)


def shape_of(shape, dtype):
    return jax.ShapeDtypeStruct(shape, dtype)


def per_device(vectors, blocks, row_blocks, col_blocks):
    stored = blocks.reshape(STEPS * SLOTS, BS, BS)
    lists = lax.all_gather(jnp.stack([row_blocks[0, 0], col_blocks[0, 0]]), "core")
    far = routed(lists, -1, -2)
    far3 = routed(lists, -3, -3)
    me = lax.axis_index("core")
    given = lax.dynamic_slice_in_dim(stored, (2 - me) * SLOTS, SLOTS, 0)
    other = lax.ppermute(given, "core", [(0, 1), (1, 0)])
    mine = pl.pallas_call(
        prepared,
        out_shape=shape_of((COL * CHUNK, HALF), BF16),
        in_specs=[VM],
        out_specs=VM,
        compiler_params=PARAMS,
    )(vectors)
    held = exchanged(mine, CHUNK)
    one = shape_of((SLOTS * NV, BS), BF16)
    two = shape_of((2, SLOTS * NV, BS), BF16)
    partials, partials3 = pl.pallas_call(
        transposed_products,
        out_shape=(two, one),
        in_specs=[SM] + [VM] * 3,
        out_specs=(VM, VM),
        compiler_params=PARAMS,
    )(lists, held, stored, other)
    back = routed(partials, -1, -2)
    back3 = routed(partials3, -3, -3)
    picked, picked3 = pl.pallas_call(
        asked_blocks,
        out_shape=(two, one),
        in_specs=[SM, SM, VM],
        out_specs=(VM, VM),
        compiler_params=PARAMS,
    )(far, far3, held)
    right = routed(picked, 1, 2)
    right3 = routed(picked3, 3, 3)
    sums = pl.pallas_call(
        own_products,
        out_shape=shape_of((COL * CHUNK, HALF), BF16),
        in_specs=[SM] * 3 + [VM] * 7,
        out_specs=VM,
        scratch_shapes=[pltpu.VMEM((NBB, NV, BS), F32)],
        compiler_params=PARAMS,
    )(lists, far, far3, held, stored, other, right, right3, back, back3)
    return pl.pallas_call(
        gathered_sum,
        out_shape=shape_of((64, NV), F32),
        in_specs=[VM],
        out_specs=VM,
        compiler_params=PARAMS,
    )(exchanged(sums, CHUNK))


def solution(mesh):
    shards, places = mesh.devices.shape
    fine = Mesh(mesh.devices.reshape(shards, places // 2, 2), AXES)
    rest = ("pos", "core")
    return jax.shard_map(
        per_device,
        mesh=fine,
        in_specs=(
            P(AXES, None),
            P("blk", rest, None, None, None, None),
            P("blk", rest, None, None),
            P("blk", rest, None, None),
        ),
        out_specs=P(AXES, None),
        check_vma=False,
    )
```

```python
import jax
import jax.numpy as jnp
from jax import lax
from jax.experimental import pallas as pl
from jax.experimental.pallas import tpu as pltpu
from jax.sharding import Mesh, PartitionSpec as P

BF16 = jnp.bfloat16
F32 = jnp.float32
COL = 64
NBB = 16
NV = 64
BS = 256
STEPS = 4
AXES = ("blk", "pos", "core")
SLOTS = 2
HALF = 128
CHUNK = 32


def routed(block, near, far):
    sizes = [lax.axis_size(axis) for axis in AXES]
    n, positions, cores = sizes
    route = []
    for shard in range(n):
        for place in range(positions * cores):
            step = far if place % cores else near
            route.append((shard * positions * cores + place, (shard + step) % n * positions * cores + place))
    return lax.ppermute(block, AXES, route)


def exchanged(flat, rows, axes):
    pieces = lax.all_to_all(flat.reshape(-1, rows, HALF), axes, 0, 0, tiled=True)
    return pieces.reshape(-1, HALF)


def dense_block(held, index):
    tops, bottoms = [], []
    for quarter in range(4):
        start = pl.multiple_of((index * 4 + quarter) * CHUNK, CHUNK)
        piece = held[pl.ds(start, CHUNK), :]
        tops.append(piece[:, :64])
        bottoms.append(piece[:, 64:])
    top = jnp.concatenate(tops, axis=1)
    bottom = jnp.concatenate(bottoms, axis=1)
    return jnp.concatenate([top, bottom], axis=0)


def times(left, block):
    return lax.dot_general(left, block, (((1,), (0,)), ((), ())), preferred_element_type=F32)


def times_transposed(left, block):
    return lax.dot_general(left, block, (((1,), (1,)), ((), ())), preferred_element_type=F32)


def prepared(vectors, out):
    rows = vectors[...]
    turned = jnp.transpose(jnp.concatenate([rows, rows], axis=1))
    packed = jnp.concatenate([turned[:32], turned[32:64]], axis=1).astype(BF16)
    for i in range(COL):
        out[i * CHUNK : (i + 1) * CHUNK, :] = packed


def shared_block(blocks, other, step, core, at):
    if core == 0:
        return blocks[step * SLOTS + at % SLOTS]
    return other[at]


def transposed_products(lists, held, blocks, other, partials):
    me = lax.axis_index("core")
    for k in range(SLOTS):
        part = slice(NV * k, NV * (k + 1))
        for core, owner in enumerate((me, 1 - me)):
            left = dense_block(held, lists[owner, 0, 1 + me, k])
            partials[core, part, :] = times(left, shared_block(blocks, other, 1 + me, core, k)).astype(BF16)


def asked_blocks(lists, far, far3, held, blocks, other, picked, third):
    me = lax.axis_index("core")
    for k in range(SLOTS):
        part = slice(NV * k, NV * (k + 1))
        for core, owner in enumerate((me, 1 - me)):
            picked[core, part, :] = dense_block(held, far[owner, 1, 1 + me, k])

    @pl.when(me == 0)
    def _():
        for k in range(SLOTS):
            for core in range(2):
                third[core, NV * k : NV * (k + 1), :] = dense_block(held, far3[core, 1, 3, k])

    @pl.when(me == 1)
    def _():
        for k in range(SLOTS):
            for core in range(2):
                left = dense_block(held, lists[1 - core, 0, 3, k])
                product = times(left, shared_block(blocks, other, 3, core, SLOTS + k))
                third[1 - core, NV * k : NV * (k + 1), :] = product.astype(BF16)


def own_products(lists, far, far3, held, blocks, other, right, back, third, out, total):
    me = lax.axis_index("core")
    total[...] = jnp.zeros_like(total)
    for k in range(SLOTS):
        part = slice(NV * k, NV * (k + 1))
        row, col = lists[me, 0, 0, k], lists[me, 1, 0, k]
        total[row] += times_transposed(dense_block(held, col), blocks[k])
        total[col] += times(dense_block(held, row), blocks[k])
        for core, owner in enumerate((me, 1 - me)):
            block = shared_block(blocks, other, 1 + me, core, k)
            total[lists[owner, 0, 1 + me, k]] += times_transposed(right[core, part, :], block)
            total[far[owner, 1, 1 + me, k]] += back[core, part, :].astype(F32)

    @pl.when(me == 0)
    def _():
        for k in range(SLOTS):
            for core in range(2):
                came = third[core, NV * k : NV * (k + 1), :]
                block = shared_block(blocks, other, 3, core, SLOTS + k)
                total[lists[core, 0, 3, k]] += times_transposed(came, block)

    @pl.when(me == 1)
    def _():
        for k in range(SLOTS):
            for core in range(2):
                total[far3[core, 1, 3, k]] += third[core, NV * k : NV * (k + 1), :].astype(F32)

    for row in range(NBB):
        whole = total[row]
        for q in range(4):
            part = whole[:, 64 * q : 64 * q + 64]
            start = ((q % 2) * (COL // 2) + row * 2 + q // 2) * CHUNK
            out[start : start + CHUNK, :] = jnp.concatenate([part[:32], part[32:]], axis=1)


def both_cores(pair, out):
    out[...] = (pair[: COL // 2 * CHUNK, :] + pair[COL // 2 * CHUNK :, :]).astype(BF16)


def gathered_sum(arrived, out):
    sums = [arrived[i * CHUNK : (i + 1) * CHUNK, :].astype(F32) for i in range(4)]
    for i in range(4, COL // 2):
        sums[i % 4] += arrived[i * CHUNK : (i + 1) * CHUNK, :].astype(F32)
    packed = (sums[0] + sums[1]) + (sums[2] + sums[3])
    own = jnp.concatenate([packed[:, :64], packed[:, 64:]], axis=0)
    out[...] = jnp.transpose(jnp.concatenate([own, own], axis=1))[:64]


VM = pl.BlockSpec(memory_space=pltpu.VMEM)
SM = pl.BlockSpec(memory_space=pltpu.SMEM)
PARAMS = pltpu.CompilerParams(vmem_limit_bytes=24 * 1024 * 1024)


def shape_of(shape, dtype):
    return jax.ShapeDtypeStruct(shape, dtype)


def per_device(vectors, blocks, row_blocks, col_blocks):
    stored = blocks.reshape(STEPS * SLOTS, BS, BS)
    lists = lax.all_gather(jnp.stack([row_blocks[0, 0], col_blocks[0, 0]]), "core")
    far = routed(lists, -1, -2)
    far3 = routed(lists, -3, -3)
    me = lax.axis_index("core")
    given = lax.dynamic_slice_in_dim(stored, (2 - me) * SLOTS, SLOTS, 0)
    given = jnp.concatenate([given, stored[3 * SLOTS :]], axis=0)
    other = lax.ppermute(given, "core", [(0, 1), (1, 0)])
    mine = pl.pallas_call(
        prepared,
        out_shape=shape_of((COL * CHUNK, HALF), BF16),
        in_specs=[VM],
        out_specs=VM,
        compiler_params=PARAMS,
    )(vectors)
    held = exchanged(mine, CHUNK, ("pos", "core"))
    two = shape_of((2, SLOTS * NV, BS), BF16)
    partials = pl.pallas_call(
        transposed_products,
        out_shape=two,
        in_specs=[SM] + [VM] * 3,
        out_specs=VM,
        compiler_params=PARAMS,
    )(lists, held, stored, other)
    back = routed(partials, -1, -2)
    picked, third = pl.pallas_call(
        asked_blocks,
        out_shape=(two, two),
        in_specs=[SM] * 3 + [VM] * 3,
        out_specs=(VM, VM),
        compiler_params=PARAMS,
    )(lists, far, far3, held, stored, other)
    right = routed(picked, 1, 2)
    third = routed(third, 3, -3)
    sums = pl.pallas_call(
        own_products,
        out_shape=shape_of((COL * CHUNK, HALF), F32),
        in_specs=[SM] * 3 + [VM] * 6,
        out_specs=VM,
        scratch_shapes=[pltpu.VMEM((NBB, NV, BS), F32)],
        compiler_params=PARAMS,
    )(lists, far, far3, held, stored, other, right, back, third)
    chips = pl.pallas_call(
        both_cores,
        out_shape=shape_of((COL // 2 * CHUNK, HALF), BF16),
        in_specs=[VM],
        out_specs=VM,
        compiler_params=PARAMS,
    )(exchanged(sums, COL // 2 * CHUNK, "core"))
    return pl.pallas_call(
        gathered_sum,
        out_shape=shape_of((64, NV), F32),
        in_specs=[VM],
        out_specs=VM,
        compiler_params=PARAMS,
    )(exchanged(chips, CHUNK, "pos"))


def solution(mesh):
    shards, places = mesh.devices.shape
    fine = Mesh(mesh.devices.reshape(shards, places // 2, 2), AXES)
    rest = ("pos", "core")
    return jax.shard_map(
        per_device,
        mesh=fine,
        in_specs=(
            P(AXES, None),
            P("blk", rest, None, None, None, None),
            P("blk", rest, None, None),
            P("blk", rest, None, None),
        ),
        out_specs=P(AXES, None),
        check_vma=False,
    )
```

```python
import jax
import jax.numpy as jnp
from jax import lax
from jax.experimental import pallas as pl
from jax.experimental.pallas import tpu as pltpu
from jax.sharding import Mesh, PartitionSpec as P

BF16 = jnp.bfloat16
F32 = jnp.float32
COL = 64
NBB = 16
NV = 64
BS = 256
STEPS = 4
AXES = ("blk", "pos", "core")
SLOTS = 2
HALF = 128
CHUNK = 32


def routed(block, near, far):
    sizes = [lax.axis_size(axis) for axis in AXES]
    n, positions, cores = sizes
    route = []
    for shard in range(n):
        for place in range(positions * cores):
            step = far if place % cores else near
            route.append((shard * positions * cores + place, (shard + step) % n * positions * cores + place))
    return lax.ppermute(block, AXES, route)


def exchanged(flat, rows, axes):
    pieces = lax.all_to_all(flat.reshape(-1, rows, HALF), axes, 0, 0, tiled=True)
    return pieces.reshape(-1, HALF)


def dense_block(held, index):
    tops, bottoms = [], []
    for quarter in range(4):
        place = (quarter % 2) * (COL // 2) + index * 2 + quarter // 2
        start = pl.multiple_of(place * CHUNK, CHUNK)
        piece = held[pl.ds(start, CHUNK), :]
        tops.append(piece[:, :64])
        bottoms.append(piece[:, 64:])
    top = jnp.concatenate(tops, axis=1)
    bottom = jnp.concatenate(bottoms, axis=1)
    return jnp.concatenate([top, bottom], axis=0)


def times(left, block):
    return lax.dot_general(left, block, (((1,), (0,)), ((), ())), preferred_element_type=F32)


def times_transposed(left, block):
    return lax.dot_general(left, block, (((1,), (1,)), ((), ())), preferred_element_type=F32)


def prepared(vectors, out):
    rows = vectors[...]
    turned = jnp.transpose(jnp.concatenate([rows, rows], axis=1))
    packed = jnp.concatenate([turned[:32], turned[32:64]], axis=1).astype(BF16)
    for i in range(COL // 2):
        out[i * CHUNK : (i + 1) * CHUNK, :] = packed


def shared_block(blocks, other, step, core, at):
    if core == 0:
        return blocks[step * SLOTS + at % SLOTS]
    return other[at]


def transposed_products(lists, held, blocks, other, partials):
    me = lax.axis_index("core")
    for k in range(SLOTS):
        part = slice(NV * k, NV * (k + 1))
        for core, owner in enumerate((me, 1 - me)):
            left = dense_block(held, lists[owner, 0, 1 + me, k])
            partials[core, part, :] = times(left, shared_block(blocks, other, 1 + me, core, k)).astype(BF16)


def asked_blocks(lists, far, far3, held, blocks, other, picked, third):
    me = lax.axis_index("core")
    for k in range(SLOTS):
        part = slice(NV * k, NV * (k + 1))
        for core, owner in enumerate((me, 1 - me)):
            picked[core, part, :] = dense_block(held, far[owner, 1, 1 + me, k])

    @pl.when(me == 0)
    def _():
        for k in range(SLOTS):
            for core in range(2):
                third[core, NV * k : NV * (k + 1), :] = dense_block(held, far3[core, 1, 3, k])

    @pl.when(me == 1)
    def _():
        for k in range(SLOTS):
            for core in range(2):
                left = dense_block(held, lists[1 - core, 0, 3, k])
                product = times(left, shared_block(blocks, other, 3, core, SLOTS + k))
                third[1 - core, NV * k : NV * (k + 1), :] = product.astype(BF16)


def early_sums(lists, far, held, blocks, back, total):
    me = lax.axis_index("core")
    total[...] = jnp.zeros_like(total)
    for k in range(SLOTS):
        part = slice(NV * k, NV * (k + 1))
        row, col = lists[me, 0, 0, k], lists[me, 1, 0, k]
        total[row] += times_transposed(dense_block(held, col), blocks[k])
        total[col] += times(dense_block(held, row), blocks[k])
        for core, owner in enumerate((me, 1 - me)):
            total[far[owner, 1, 1 + me, k]] += back[core, part, :].astype(F32)


def packed_rows(total, *outs):
    for row in range(NBB):
        whole = total[row]
        for q in range(4):
            part = whole[:, 64 * q : 64 * q + 64]
            start = (row * 2 + q // 2) * CHUNK
            outs[q % 2][start : start + CHUNK, :] = jnp.concatenate([part[:32], part[32:]], axis=1)


def late_sums(lists, far3, early, blocks, other, right, third, kept, given, total):
    me = lax.axis_index("core")
    total[...] = early[...]
    for k in range(SLOTS):
        part = slice(NV * k, NV * (k + 1))
        for core, owner in enumerate((me, 1 - me)):
            block = shared_block(blocks, other, 1 + me, core, k)
            total[lists[owner, 0, 1 + me, k]] += times_transposed(right[core, part, :], block)

    @pl.when(me == 0)
    def _():
        for k in range(SLOTS):
            for core in range(2):
                came = third[core, NV * k : NV * (k + 1), :]
                block = shared_block(blocks, other, 3, core, SLOTS + k)
                total[lists[core, 0, 3, k]] += times_transposed(came, block)

    @pl.when(me == 1)
    def _():
        for k in range(SLOTS):
            for core in range(2):
                total[far3[core, 1, 3, k]] += third[core, NV * k : NV * (k + 1), :].astype(F32)

    @pl.when(me == 0)
    def _():
        packed_rows(total, kept, given)

    @pl.when(me == 1)
    def _():
        packed_rows(total, given, kept)


def both_cores(kept, got, out):
    out[...] = (kept[...] + got[...]).astype(BF16)


def gathered_sum(arrived, out):
    sums = [arrived[i * CHUNK : (i + 1) * CHUNK, :].astype(F32) for i in range(4)]
    for i in range(4, COL // 2):
        sums[i % 4] += arrived[i * CHUNK : (i + 1) * CHUNK, :].astype(F32)
    packed = (sums[0] + sums[1]) + (sums[2] + sums[3])
    own = jnp.concatenate([packed[:, :64], packed[:, 64:]], axis=0)
    out[...] = jnp.transpose(jnp.concatenate([own, own], axis=1))[:64]


VM = pl.BlockSpec(memory_space=pltpu.VMEM)
SM = pl.BlockSpec(memory_space=pltpu.SMEM)
PARAMS = pltpu.CompilerParams(vmem_limit_bytes=24 * 1024 * 1024)


def shape_of(shape, dtype):
    return jax.ShapeDtypeStruct(shape, dtype)


def per_device(vectors, blocks, row_blocks, col_blocks):
    stored = blocks.reshape(STEPS * SLOTS, BS, BS)
    lists = lax.all_gather(jnp.stack([row_blocks[0, 0], col_blocks[0, 0]]), "core")
    far = routed(lists, -1, -2)
    far3 = routed(lists, -3, -3)
    me = lax.axis_index("core")
    given = lax.dynamic_slice_in_dim(stored, (2 - me) * SLOTS, SLOTS, 0)
    given = jnp.concatenate([given, stored[3 * SLOTS :]], axis=0)
    other = lax.ppermute(given, "core", [(0, 1), (1, 0)])
    mine = pl.pallas_call(
        prepared,
        out_shape=shape_of((COL // 2 * CHUNK, HALF), BF16),
        in_specs=[VM],
        out_specs=VM,
        compiler_params=PARAMS,
    )(vectors)
    held = lax.all_gather(exchanged(mine, CHUNK, "pos"), "core", tiled=True)
    two = shape_of((2, SLOTS * NV, BS), BF16)
    partials = pl.pallas_call(
        transposed_products,
        out_shape=two,
        in_specs=[SM] + [VM] * 3,
        out_specs=VM,
        compiler_params=PARAMS,
    )(lists, held, stored, other)
    back = routed(partials, -1, -2)
    picked, third = pl.pallas_call(
        asked_blocks,
        out_shape=(two, two),
        in_specs=[SM] * 3 + [VM] * 3,
        out_specs=(VM, VM),
        compiler_params=PARAMS,
    )(lists, far, far3, held, stored, other)
    right = routed(picked, 1, 2)
    third = routed(third, 3, -3)
    early = pl.pallas_call(
        early_sums,
        out_shape=shape_of((NBB, NV, BS), F32),
        in_specs=[SM] * 2 + [VM] * 3,
        out_specs=VM,
        compiler_params=PARAMS,
    )(lists, far, held, stored, back)
    half = shape_of((COL // 2 * CHUNK, HALF), F32)
    kept, given = pl.pallas_call(
        late_sums,
        out_shape=(half, half),
        in_specs=[SM] * 2 + [VM] * 5,
        out_specs=(VM, VM),
        scratch_shapes=[pltpu.VMEM((NBB, NV, BS), F32)],
        compiler_params=PARAMS,
    )(lists, far3, early, stored, other, right, third)
    chips = pl.pallas_call(
        both_cores,
        out_shape=shape_of((COL // 2 * CHUNK, HALF), BF16),
        in_specs=[VM, VM],
        out_specs=VM,
        compiler_params=PARAMS,
    )(kept, lax.ppermute(given, "core", [(0, 1), (1, 0)]))
    return pl.pallas_call(
        gathered_sum,
        out_shape=shape_of((64, NV), F32),
        in_specs=[VM],
        out_specs=VM,
        compiler_params=PARAMS,
    )(exchanged(chips, CHUNK, "pos"))


def solution(mesh):
    shards, places = mesh.devices.shape
    fine = Mesh(mesh.devices.reshape(shards, places // 2, 2), AXES)
    rest = ("pos", "core")
    return jax.shard_map(
        per_device,
        mesh=fine,
        in_specs=(
            P(AXES, None),
            P("blk", rest, None, None, None, None),
            P("blk", rest, None, None),
            P("blk", rest, None, None),
        ),
        out_specs=P(AXES, None),
        check_vma=False,
    )
```

```python
import jax
import jax.numpy as jnp
from jax import lax
from jax.experimental import pallas as pl
from jax.experimental.pallas import tpu as pltpu
from jax.sharding import Mesh, PartitionSpec as P

BF16 = jnp.bfloat16
F32 = jnp.float32
COL = 64
NBB = 16
NV = 64
BS = 256
STEPS = 4
AXES = ("blk", "pos", "core")
SLOTS = 2
HALF = 128
CHUNK = 32


def routed(block, near, far):
    sizes = [lax.axis_size(axis) for axis in AXES]
    n, positions, cores = sizes
    route = []
    for shard in range(n):
        for place in range(positions * cores):
            step = far if place % cores else near
            route.append((shard * positions * cores + place, (shard + step) % n * positions * cores + place))
    return lax.ppermute(block, AXES, route)


def exchanged(flat, rows, axes):
    pieces = lax.all_to_all(flat.reshape(-1, rows, HALF), axes, 0, 0, tiled=True)
    return pieces.reshape(-1, HALF)


def dense_block(held, index):
    tops, bottoms = [], []
    for quarter in range(4):
        place = (quarter % 2) * (COL // 2) + index * 2 + quarter // 2
        start = pl.multiple_of(place * CHUNK, CHUNK)
        piece = held[pl.ds(start, CHUNK), :]
        tops.append(piece[:, :64])
        bottoms.append(piece[:, 64:])
    top = jnp.concatenate(tops, axis=1)
    bottom = jnp.concatenate(bottoms, axis=1)
    return jnp.concatenate([top, bottom], axis=0)


def times(left, block):
    return lax.dot_general(left, block, (((1,), (0,)), ((), ())), preferred_element_type=F32)


def times_transposed(left, block):
    return lax.dot_general(left, block, (((1,), (1,)), ((), ())), preferred_element_type=F32)


def prepared(vectors, out):
    rows = vectors[...]
    turned = jnp.transpose(jnp.concatenate([rows, rows], axis=1))
    packed = jnp.concatenate([turned[:32], turned[32:64]], axis=1).astype(BF16)
    for i in range(COL // 2):
        out[i * CHUNK : (i + 1) * CHUNK, :] = packed


def shared_block(blocks, other, step, core, k):
    return other[(step - 1) * SLOTS + k] if core else blocks[step * SLOTS + k]


def transposed_products(lists, held, blocks, other, partials):
    me = lax.axis_index("core")
    for k in range(SLOTS):
        part = slice(NV * k, NV * (k + 1))
        for core, owner in enumerate((me, 1 - me)):
            left = dense_block(held, lists[owner, 0, 1 + me, k])
            partials[core, part, :] = times(left, shared_block(blocks, other, 1 + me, core, k)).astype(BF16)


def asked_blocks(far, held, picked):
    me = lax.axis_index("core")
    for k in range(SLOTS):
        for core, owner in enumerate((me, 1 - me)):
            picked[core, NV * k : NV * (k + 1), :] = dense_block(held, far[owner, 1, 1 + me, k])


def third_blocks(lists, far3, held, blocks, other, third):
    me = lax.axis_index("core")

    @pl.when(me == 0)
    def _():
        for k in range(SLOTS):
            for core in range(2):
                third[core, NV * k : NV * (k + 1), :] = dense_block(held, far3[core, 1, 3, k])

    @pl.when(me == 1)
    def _():
        for k in range(SLOTS):
            for core in range(2):
                left = dense_block(held, lists[1 - core, 0, 3, k])
                product = times(left, shared_block(blocks, other, 3, core, k))
                third[1 - core, NV * k : NV * (k + 1), :] = product.astype(BF16)


def early_sums(lists, far, held, blocks, back, total):
    me = lax.axis_index("core")
    total[...] = jnp.zeros_like(total)
    for k in range(SLOTS):
        part = slice(NV * k, NV * (k + 1))
        row, col = lists[me, 0, 0, k], lists[me, 1, 0, k]
        total[row] += times_transposed(dense_block(held, col), blocks[k])
        total[col] += times(dense_block(held, row), blocks[k])
        for core, owner in enumerate((me, 1 - me)):
            total[far[owner, 1, 1 + me, k]] += back[core, part, :].astype(F32)


def packed_rows(total, *outs):
    for row in range(NBB):
        whole = total[row]
        for q in range(4):
            part = whole[:, 64 * q : 64 * q + 64]
            start = (row * 2 + q // 2) * CHUNK
            outs[q % 2][start : start + CHUNK, :] = jnp.concatenate([part[:32], part[32:]], axis=1)


def late_sums(lists, far3, early, blocks, other, right, third, kept, given, total):
    me = lax.axis_index("core")
    for k in range(SLOTS):
        part = slice(NV * k, NV * (k + 1))
        for core, owner in enumerate((me, 1 - me)):
            block = shared_block(blocks, other, 1 + me, core, k)
            total[lists[owner, 0, 1 + me, k]] += times_transposed(right[core, part, :], block)

    @pl.when(me == 0)
    def _():
        for k in range(SLOTS):
            for core in range(2):
                came = third[core, NV * k : NV * (k + 1), :]
                block = shared_block(blocks, other, 3, core, k)
                total[lists[core, 0, 3, k]] += times_transposed(came, block)

    @pl.when(me == 1)
    def _():
        for k in range(SLOTS):
            for core in range(2):
                total[far3[core, 1, 3, k]] += third[core, NV * k : NV * (k + 1), :].astype(F32)

    @pl.when(me == 0)
    def _():
        packed_rows(total, kept, given)

    @pl.when(me == 1)
    def _():
        packed_rows(total, given, kept)


def both_cores(kept, got, out):
    out[...] = (kept[...] + got[...]).astype(BF16)


def gathered_sum(arrived, out):
    sums = [arrived[i * CHUNK : (i + 1) * CHUNK, :].astype(F32) for i in range(4)]
    for i in range(4, COL // 2):
        sums[i % 4] += arrived[i * CHUNK : (i + 1) * CHUNK, :].astype(F32)
    packed = (sums[0] + sums[1]) + (sums[2] + sums[3])
    own = jnp.concatenate([packed[:, :64], packed[:, 64:]], axis=0)
    out[...] = jnp.transpose(jnp.concatenate([own, own], axis=1))[:64]


VM = pl.BlockSpec(memory_space=pltpu.VMEM)
SM = pl.BlockSpec(memory_space=pltpu.SMEM)
PARAMS = pltpu.CompilerParams(vmem_limit_bytes=24 * 1024 * 1024)


def shape_of(shape, dtype):
    return jax.ShapeDtypeStruct(shape, dtype)


def per_device(vectors, blocks, row_blocks, col_blocks):
    stored = blocks.reshape(STEPS * SLOTS, BS, BS)
    mine = pl.pallas_call(
        prepared,
        out_shape=shape_of((COL // 2 * CHUNK, HALF), BF16),
        in_specs=[VM],
        out_specs=VM,
        compiler_params=PARAMS,
    )(vectors)
    arriving = exchanged(mine, CHUNK, "pos")
    lists = lax.all_gather(jnp.stack([row_blocks[0, 0], col_blocks[0, 0]]), "core")
    far = routed(lists, -1, -2)
    other = lax.ppermute(stored[SLOTS:], "core", [(0, 1), (1, 0)])
    held = lax.all_gather(arriving, "core", tiled=True)
    two = shape_of((2, SLOTS * NV, BS), BF16)
    partials = pl.pallas_call(
        transposed_products,
        out_shape=two,
        in_specs=[SM] + [VM] * 3,
        out_specs=VM,
        compiler_params=PARAMS,
    )(lists, held, stored, other)
    back = routed(partials, -1, -2)
    later_lists, later_far, _ = lax.optimization_barrier((lists, far, partials))
    far3 = routed(later_lists, -3, -3)
    picked = pl.pallas_call(
        asked_blocks,
        out_shape=two,
        in_specs=[SM, VM],
        out_specs=VM,
        compiler_params=PARAMS,
    )(later_far, held)
    right = routed(picked, 1, 2)
    third = pl.pallas_call(
        third_blocks,
        out_shape=two,
        in_specs=[SM, SM] + [VM] * 3,
        out_specs=VM,
        compiler_params=PARAMS,
    )(lists, far3, held, stored, other)
    third = routed(third, 3, -3)
    early = pl.pallas_call(
        early_sums,
        out_shape=shape_of((NBB, NV, BS), F32),
        in_specs=[SM] * 2 + [VM] * 3,
        out_specs=VM,
        compiler_params=PARAMS,
    )(lists, far, held, stored, back)
    half = shape_of((COL // 2 * CHUNK, HALF), F32)
    kept, given, _ = pl.pallas_call(
        late_sums,
        out_shape=(half, half, shape_of((NBB, NV, BS), F32)),
        in_specs=[SM] * 2 + [VM] * 5,
        out_specs=(VM,) * 3,
        input_output_aliases={2: 2},
        compiler_params=PARAMS,
    )(lists, far3, early, stored, other, right, third)
    chips = pl.pallas_call(
        both_cores,
        out_shape=shape_of((COL // 2 * CHUNK, HALF), BF16),
        in_specs=[VM, VM],
        out_specs=VM,
        compiler_params=PARAMS,
    )(kept, lax.ppermute(given, "core", [(0, 1), (1, 0)]))
    return pl.pallas_call(
        gathered_sum,
        out_shape=shape_of((64, NV), F32),
        in_specs=[VM],
        out_specs=VM,
        compiler_params=PARAMS,
    )(exchanged(chips, CHUNK, "pos"))


def solution(mesh):
    shards, places = mesh.devices.shape
    fine = Mesh(mesh.devices.reshape(shards, places // 2, 2), AXES)
    rest = ("pos", "core")
    return jax.shard_map(
        per_device,
        mesh=fine,
        in_specs=(
            P(AXES, None),
            P("blk", rest, None, None, None, None),
            P("blk", rest, None, None),
            P("blk", rest, None, None),
        ),
        out_specs=P(AXES, None),
        check_vma=False,
    )
```

```python
import jax
import jax.numpy as jnp
from jax import lax
from jax.experimental import pallas as pl
from jax.experimental.pallas import tpu as pltpu
from jax.sharding import Mesh, PartitionSpec as P

BF16 = jnp.bfloat16
F32 = jnp.float32
COL = 64
NBB = 16
NV = 64
BS = 256
STEPS = 4
AXES = ("blk", "pos", "core")
SLOTS = 2
HALF = 128
CHUNK = 32


def routed(block, near, far):
    sizes = [lax.axis_size(axis) for axis in AXES]
    n, positions, cores = sizes
    route = []
    for shard in range(n):
        for place in range(positions * cores):
            step = far if place % cores else near
            route.append((shard * positions * cores + place, (shard + step) % n * positions * cores + place))
    return lax.ppermute(block, AXES, route)


def exchanged(flat, rows, axes):
    pieces = lax.all_to_all(flat.reshape(-1, rows, HALF), axes, 0, 0, tiled=True)
    return pieces.reshape(-1, HALF)


def dense_block(held, index):
    tops, bottoms = [], []
    for quarter in range(4):
        place = (quarter % 2) * (COL // 2) + index * 2 + quarter // 2
        start = pl.multiple_of(place * CHUNK, CHUNK)
        piece = held[pl.ds(start, CHUNK), :]
        tops.append(piece[:, :64])
        bottoms.append(piece[:, 64:])
    top = jnp.concatenate(tops, axis=1)
    bottom = jnp.concatenate(bottoms, axis=1)
    return jnp.concatenate([top, bottom], axis=0)


def times(left, block):
    return lax.dot_general(left, block, (((1,), (0,)), ((), ())), preferred_element_type=F32)


def times_transposed(left, block):
    return lax.dot_general(left, block, (((1,), (1,)), ((), ())), preferred_element_type=F32)


def prepared(vectors, out):
    rows = vectors[...]
    turned = jnp.transpose(jnp.concatenate([rows, rows], axis=1))
    packed = jnp.concatenate([turned[:32], turned[32:64]], axis=1).astype(BF16)
    for i in range(COL // 2):
        out[i * CHUNK : (i + 1) * CHUNK, :] = packed


def shared_block(blocks, other, step, core, k):
    return (other if core else blocks)[step * SLOTS + k]


def transposed_products(lists, held, blocks, other, partials):
    me = lax.axis_index("core")
    for k in range(SLOTS):
        part = slice(NV * k, NV * (k + 1))
        for core, owner in enumerate((me, 1 - me)):
            left = dense_block(held, lists[owner, 0, 1 + me, k])
            partials[core, part, :] = times(left, shared_block(blocks, other, 1 + me, core, k)).astype(BF16)


def asked_blocks(far, held, picked):
    me = lax.axis_index("core")
    for k in range(SLOTS):
        for core, owner in enumerate((me, 1 - me)):
            picked[core, NV * k : NV * (k + 1), :] = dense_block(held, far[owner, 1, 1 + me, k])


def third_blocks(lists, far3, held, blocks, other, third):
    me = lax.axis_index("core")

    @pl.when(me == 0)
    def _():
        for k in range(SLOTS):
            for core in range(2):
                third[core, NV * k : NV * (k + 1), :] = dense_block(held, far3[core, 1, 3, k])

    @pl.when(me == 1)
    def _():
        for k in range(SLOTS):
            for core in range(2):
                left = dense_block(held, lists[1 - core, 0, 3, k])
                product = times(left, shared_block(blocks, other, 3, core, k))
                third[1 - core, NV * k : NV * (k + 1), :] = product.astype(BF16)


def early_sums(lists, far, held, blocks, back, total):
    me = lax.axis_index("core")
    total[...] = jnp.zeros_like(total)
    for k in range(SLOTS):
        part = slice(NV * k, NV * (k + 1))
        row, col = lists[me, 0, 0, k], lists[me, 1, 0, k]
        total[row] += times_transposed(dense_block(held, col), blocks[k])
        total[col] += times(dense_block(held, row), blocks[k])
        for core, owner in enumerate((me, 1 - me)):
            total[far[owner, 1, 1 + me, k]] += back[core, part, :].astype(F32)


def packed_rows(total, *outs):
    for row in range(NBB):
        whole = total[row]
        for q in range(4):
            part = whole[:, 64 * q : 64 * q + 64]
            start = (row * 2 + q // 2) * CHUNK
            outs[q % 2][start : start + CHUNK, :] = jnp.concatenate([part[:32], part[32:]], axis=1)


def late_sums(lists, far3, early, blocks, other, right, third, kept, given, total):
    me = lax.axis_index("core")
    for k in range(SLOTS):
        part = slice(NV * k, NV * (k + 1))
        for core, owner in enumerate((me, 1 - me)):
            block = shared_block(blocks, other, 1 + me, core, k)
            total[lists[owner, 0, 1 + me, k]] += times_transposed(right[core, part, :], block)

    @pl.when(me == 0)
    def _():
        for k in range(SLOTS):
            for core in range(2):
                came = third[core, NV * k : NV * (k + 1), :]
                block = shared_block(blocks, other, 3, core, k)
                total[lists[core, 0, 3, k]] += times_transposed(came, block)

    @pl.when(me == 1)
    def _():
        for k in range(SLOTS):
            for core in range(2):
                total[far3[core, 1, 3, k]] += third[core, NV * k : NV * (k + 1), :].astype(F32)

    @pl.when(me == 0)
    def _():
        packed_rows(total, kept, given)

    @pl.when(me == 1)
    def _():
        packed_rows(total, given, kept)


def both_cores(kept, got, out):
    out[...] = (kept[...] + got[...]).astype(BF16)


def gathered_sum(arrived, out):
    sums = [arrived[i * CHUNK : (i + 1) * CHUNK, :].astype(F32) for i in range(4)]
    for i in range(4, COL // 2):
        sums[i % 4] += arrived[i * CHUNK : (i + 1) * CHUNK, :].astype(F32)
    packed = (sums[0] + sums[1]) + (sums[2] + sums[3])
    own = jnp.concatenate([packed[:, :64], packed[:, 64:]], axis=0)
    out[...] = jnp.transpose(jnp.concatenate([own, own], axis=1))[:64]


VM = pl.BlockSpec(memory_space=pltpu.VMEM)
SM = pl.BlockSpec(memory_space=pltpu.SMEM)
PARAMS = pltpu.CompilerParams(vmem_limit_bytes=24 * 1024 * 1024)


def shape_of(shape, dtype):
    return jax.ShapeDtypeStruct(shape, dtype)


def per_device(vectors, blocks, row_blocks, col_blocks):
    stored = blocks.reshape(STEPS * SLOTS, BS, BS)
    mine = pl.pallas_call(
        prepared,
        out_shape=shape_of((COL // 2 * CHUNK, HALF), BF16),
        in_specs=[VM],
        out_specs=VM,
        compiler_params=PARAMS,
    )(vectors)
    arriving = exchanged(mine, CHUNK, "pos")
    lists = lax.all_gather(jnp.stack([row_blocks[0, 0], col_blocks[0, 0]]), "core")
    far = routed(lists, -1, -2)
    other = lax.ppermute(stored, "core", [(0, 1), (1, 0)])
    held = lax.all_gather(arriving, "core", tiled=True)
    two = shape_of((2, SLOTS * NV, BS), BF16)
    partials = pl.pallas_call(
        transposed_products,
        out_shape=two,
        in_specs=[SM] + [VM] * 3,
        out_specs=VM,
        compiler_params=PARAMS,
    )(lists, held, stored, other)
    back = routed(partials, -1, -2)
    later_far, _ = lax.optimization_barrier((far, partials))
    far3 = routed(lists, -3, -3)
    picked = pl.pallas_call(
        asked_blocks,
        out_shape=two,
        in_specs=[SM, VM],
        out_specs=VM,
        compiler_params=PARAMS,
    )(later_far, held)
    right = routed(picked, 1, 2)
    third = pl.pallas_call(
        third_blocks,
        out_shape=two,
        in_specs=[SM, SM] + [VM] * 3,
        out_specs=VM,
        compiler_params=PARAMS,
    )(lists, far3, held, stored, other)
    third_sent = third
    third = routed(third, 3, -3)
    early = pl.pallas_call(
        early_sums,
        out_shape=shape_of((NBB, NV, BS), F32),
        in_specs=[SM] * 2 + [VM] * 3,
        out_specs=VM,
        compiler_params=PARAMS,
    )(lists, far, lax.optimization_barrier((held, third_sent))[0], stored, back)
    half = shape_of((COL // 2 * CHUNK, HALF), F32)
    kept, given, _ = pl.pallas_call(
        late_sums,
        out_shape=(half, half, shape_of((NBB, NV, BS), F32)),
        in_specs=[SM] * 2 + [VM] * 5,
        out_specs=(VM,) * 3,
        input_output_aliases={2: 2},
        compiler_params=PARAMS,
    )(lists, far3, early, stored, other, right, third)
    chips = pl.pallas_call(
        both_cores,
        out_shape=shape_of((COL // 2 * CHUNK, HALF), BF16),
        in_specs=[VM, VM],
        out_specs=VM,
        compiler_params=PARAMS,
    )(kept, lax.ppermute(given, "core", [(0, 1), (1, 0)]))
    return pl.pallas_call(
        gathered_sum,
        out_shape=shape_of((64, NV), F32),
        in_specs=[VM],
        out_specs=VM,
        compiler_params=PARAMS,
    )(exchanged(chips, CHUNK, "pos"))


def solution(mesh):
    shards, places = mesh.devices.shape
    fine = Mesh(mesh.devices.reshape(shards, places // 2, 2), AXES)
    rest = ("pos", "core")
    return jax.shard_map(
        per_device,
        mesh=fine,
        in_specs=(
            P(AXES, None),
            P("blk", rest, None, None, None, None),
            P("blk", rest, None, None),
            P("blk", rest, None, None),
        ),
        out_specs=P(AXES, None),
        check_vma=False,
    )
```

```python
import jax
import jax.numpy as jnp
from jax import lax
from jax.experimental import pallas as pl
from jax.experimental.pallas import tpu as pltpu
from jax.sharding import Mesh, PartitionSpec as P

BF16 = jnp.bfloat16
F32 = jnp.float32
COL = 64
NBB = 16
NV = 64
BS = 256
STEPS = 4
AXES = ("blk", "pos", "core")
SLOTS = 2
HALF = 128
CHUNK = 32


def routed(block, near, far):
    sizes = [lax.axis_size(axis) for axis in AXES]
    n, positions, cores = sizes
    route = []
    for shard in range(n):
        for place in range(positions * cores):
            step = far if place % cores else near
            route.append((shard * positions * cores + place, (shard + step) % n * positions * cores + place))
    return lax.ppermute(block, AXES, route)


def exchanged(flat, rows, axes):
    pieces = lax.all_to_all(flat.reshape(-1, rows, HALF), axes, 0, 0, tiled=True)
    return pieces.reshape(-1, HALF)


def dense_block(held, index):
    tops, bottoms = [], []
    for quarter in range(4):
        place = (quarter % 2) * (COL // 2) + index * 2 + quarter // 2
        start = pl.multiple_of(place * CHUNK, CHUNK)
        piece = held[pl.ds(start, CHUNK), :]
        tops.append(piece[:, :64])
        bottoms.append(piece[:, 64:])
    top = jnp.concatenate(tops, axis=1)
    bottom = jnp.concatenate(bottoms, axis=1)
    return jnp.concatenate([top, bottom], axis=0)


def times(left, block):
    return lax.dot_general(left, block, (((1,), (0,)), ((), ())), preferred_element_type=F32)


def times_transposed(left, block):
    return lax.dot_general(left, block, (((1,), (1,)), ((), ())), preferred_element_type=F32)


def prepared(vectors, out):
    rows = vectors[...]
    turned = jnp.transpose(jnp.concatenate([rows, rows], axis=1))
    packed = jnp.concatenate([turned[:32], turned[32:64]], axis=1).astype(BF16)
    for i in range(COL // 2):
        out[i * CHUNK : (i + 1) * CHUNK, :] = packed


def shared_block(blocks, other, step, core, k):
    return (other if core else blocks)[step * SLOTS + k]


def transposed_products(lists, held, blocks, other, partials):
    me = lax.axis_index("core")
    for k in range(SLOTS):
        part = slice(NV * k, NV * (k + 1))
        for core, owner in enumerate((me, 1 - me)):
            left = dense_block(held, lists[owner, 0, 1 + me, k])
            partials[core, part, :] = times(left, shared_block(blocks, other, 1 + me, core, k)).astype(BF16)


def asked_blocks(far, held, picked):
    me = lax.axis_index("core")
    for k in range(SLOTS):
        for core, owner in enumerate((me, 1 - me)):
            picked[core, NV * k : NV * (k + 1), :] = dense_block(held, far[owner, 1, 1 + me, k])


def third_blocks(lists, far3, held, blocks, other, third):
    me = lax.axis_index("core")

    @pl.when(me == 0)
    def _():
        for k in range(SLOTS):
            for core in range(2):
                third[core, NV * k : NV * (k + 1), :] = dense_block(held, far3[core, 1, 3, k])

    @pl.when(me == 1)
    def _():
        for k in range(SLOTS):
            for core in range(2):
                left = dense_block(held, lists[1 - core, 0, 3, k])
                product = times(left, shared_block(blocks, other, 3, core, k))
                third[1 - core, NV * k : NV * (k + 1), :] = product.astype(BF16)


def early_sums(lists, far, held, blocks, back, total):
    me = lax.axis_index("core")
    total[...] = jnp.zeros_like(total)
    for k in range(SLOTS):
        part = slice(NV * k, NV * (k + 1))
        row, col = lists[me, 0, 0, k], lists[me, 1, 0, k]
        total[row] += times_transposed(dense_block(held, col), blocks[k])
        total[col] += times(dense_block(held, row), blocks[k])
        for core, owner in enumerate((me, 1 - me)):
            total[far[owner, 1, 1 + me, k]] += back[core, part, :].astype(F32)


def packed_rows(total, *outs):
    for row in range(NBB):
        whole = total[row]
        for q in range(4):
            part = whole[:, 64 * q : 64 * q + 64]
            start = (row * 2 + q // 2) * CHUNK
            out = outs[q % 2]
            out[start : start + CHUNK, :] = jnp.concatenate([part[:32], part[32:]], axis=1).astype(out.dtype)


def late_sums(lists, far3, early, blocks, other, right, third, kept, given, total):
    me = lax.axis_index("core")
    for k in range(SLOTS):
        part = slice(NV * k, NV * (k + 1))
        for core, owner in enumerate((me, 1 - me)):
            block = shared_block(blocks, other, 1 + me, core, k)
            total[lists[owner, 0, 1 + me, k]] += times_transposed(right[core, part, :], block)

    @pl.when(me == 0)
    def _():
        for k in range(SLOTS):
            for core in range(2):
                came = third[core, NV * k : NV * (k + 1), :]
                block = shared_block(blocks, other, 3, core, k)
                total[lists[core, 0, 3, k]] += times_transposed(came, block)

    @pl.when(me == 1)
    def _():
        for k in range(SLOTS):
            for core in range(2):
                total[far3[core, 1, 3, k]] += third[core, NV * k : NV * (k + 1), :].astype(F32)

    @pl.when(me == 0)
    def _():
        packed_rows(total, kept, given)

    @pl.when(me == 1)
    def _():
        packed_rows(total, given, kept)


def both_cores(kept, got, out):
    theirs = got[1 - lax.axis_index("core")]
    out[...] = (kept[...] + theirs.astype(F32)).astype(BF16)


def gathered_sum(arrived, out):
    sums = [arrived[i * CHUNK : (i + 1) * CHUNK, :].astype(F32) for i in range(4)]
    for i in range(4, COL // 2):
        sums[i % 4] += arrived[i * CHUNK : (i + 1) * CHUNK, :].astype(F32)
    packed = (sums[0] + sums[1]) + (sums[2] + sums[3])
    own = jnp.concatenate([packed[:, :64], packed[:, 64:]], axis=0)
    out[...] = jnp.transpose(jnp.concatenate([own, own], axis=1))[:64]


VM = pl.BlockSpec(memory_space=pltpu.VMEM)
SM = pl.BlockSpec(memory_space=pltpu.SMEM)
PARAMS = pltpu.CompilerParams(vmem_limit_bytes=24 * 1024 * 1024)


def shape_of(shape, dtype):
    return jax.ShapeDtypeStruct(shape, dtype)


def per_device(vectors, blocks, row_blocks, col_blocks):
    stored = blocks.reshape(STEPS * SLOTS, BS, BS)
    mine = pl.pallas_call(
        prepared,
        out_shape=shape_of((COL // 2 * CHUNK, HALF), BF16),
        in_specs=[VM],
        out_specs=VM,
        compiler_params=PARAMS,
    )(vectors)
    arriving = exchanged(mine, CHUNK, "pos")
    lists = lax.all_gather(jnp.stack([row_blocks[0, 0], col_blocks[0, 0]]), "core")
    far = routed(lists, -1, -2)
    other = lax.ppermute(stored, "core", [(0, 1), (1, 0)])
    held = lax.all_gather(arriving, "core", tiled=True)
    two = shape_of((2, SLOTS * NV, BS), BF16)
    partials = pl.pallas_call(
        transposed_products,
        out_shape=two,
        in_specs=[SM] + [VM] * 3,
        out_specs=VM,
        compiler_params=PARAMS,
    )(lists, held, stored, other)
    back = routed(partials, -1, -2)
    later_far, _ = lax.optimization_barrier((far, partials))
    far3 = routed(lists, -3, -3)
    picked = pl.pallas_call(
        asked_blocks,
        out_shape=two,
        in_specs=[SM, VM],
        out_specs=VM,
        compiler_params=PARAMS,
    )(later_far, held)
    right = routed(picked, 1, 2)
    third = pl.pallas_call(
        third_blocks,
        out_shape=two,
        in_specs=[SM, SM] + [VM] * 3,
        out_specs=VM,
        compiler_params=PARAMS,
    )(lists, far3, held, stored, other)
    third_sent = third
    third = routed(third, 3, -3)
    early = pl.pallas_call(
        early_sums,
        out_shape=shape_of((NBB, NV, BS), F32),
        in_specs=[SM] * 2 + [VM] * 3,
        out_specs=VM,
        compiler_params=PARAMS,
    )(lists, far, lax.optimization_barrier((held, third_sent))[0], stored, back)
    half = (COL // 2 * CHUNK, HALF)
    kept, given, _ = pl.pallas_call(
        late_sums,
        out_shape=(shape_of(half, F32), shape_of(half, BF16), shape_of((NBB, NV, BS), F32)),
        in_specs=[SM] * 2 + [VM] * 5,
        out_specs=(VM,) * 3,
        input_output_aliases={2: 2},
        compiler_params=PARAMS,
    )(lists, far3, early, stored, other, right, third)
    chips = pl.pallas_call(
        both_cores,
        out_shape=shape_of(half, BF16),
        in_specs=[VM, VM],
        out_specs=VM,
        compiler_params=PARAMS,
    )(kept, lax.all_gather(given, "core"))
    return pl.pallas_call(
        gathered_sum,
        out_shape=shape_of((64, NV), F32),
        in_specs=[VM],
        out_specs=VM,
        compiler_params=PARAMS,
    )(exchanged(chips, CHUNK, "pos"))


def solution(mesh):
    shards, places = mesh.devices.shape
    fine = Mesh(mesh.devices.reshape(shards, places // 2, 2), AXES)
    rest = ("pos", "core")
    return jax.shard_map(
        per_device,
        mesh=fine,
        in_specs=(
            P(AXES, None),
            P("blk", rest, None, None, None, None),
            P("blk", rest, None, None),
            P("blk", rest, None, None),
        ),
        out_specs=P(AXES, None),
        check_vma=False,
    )
```

```python
import jax
import jax.numpy as jnp
from jax import lax
from jax.experimental import pallas as pl
from jax.experimental.pallas import tpu as pltpu
from jax.sharding import Mesh, PartitionSpec as P

BF16 = jnp.bfloat16
F32 = jnp.float32
COL = 64
NBB = 16
NV = 64
BS = 256
STEPS = 4
AXES = ("blk", "pos", "core")
SLOTS = 2
HALF = 128
CHUNK = 32


def routed(block, near, far):
    sizes = [lax.axis_size(axis) for axis in AXES]
    n, positions, cores = sizes
    route = []
    for shard in range(n):
        for place in range(positions * cores):
            step = far if place % cores else near
            route.append((shard * positions * cores + place, (shard + step) % n * positions * cores + place))
    return lax.ppermute(block, AXES, route)


def exchanged(flat, rows, axes):
    pieces = lax.all_to_all(flat.reshape(-1, rows, HALF), axes, 0, 0, tiled=True)
    return pieces.reshape(-1, HALF)


def dense_block(held, index):
    tops, bottoms = [], []
    for quarter in range(4):
        place = (quarter % 2) * (COL // 2) + index * 2 + quarter // 2
        start = pl.multiple_of(place * CHUNK, CHUNK)
        piece = held[pl.ds(start, CHUNK), :]
        tops.append(piece[:, :64])
        bottoms.append(piece[:, 64:])
    top = jnp.concatenate(tops, axis=1)
    bottom = jnp.concatenate(bottoms, axis=1)
    return jnp.concatenate([top, bottom], axis=0)


def times(left, block):
    return lax.dot_general(left, block, (((1,), (0,)), ((), ())), preferred_element_type=F32)


def times_transposed(left, block):
    return lax.dot_general(left, block, (((1,), (1,)), ((), ())), preferred_element_type=F32)


def prepared(vectors, out):
    rows = vectors[...]
    turned = jnp.transpose(jnp.concatenate([rows, rows], axis=1))
    packed = jnp.concatenate([turned[:32], turned[32:64]], axis=1).astype(BF16)
    for i in range(COL // 2):
        out[i * CHUNK : (i + 1) * CHUNK, :] = packed


def shared_block(blocks, other, step, core, k):
    return (other if core else blocks)[step * SLOTS + k]


def transposed_products(lists, held, blocks, other, partials):
    me = lax.axis_index("core")
    for k in range(SLOTS):
        part = slice(NV * k, NV * (k + 1))
        for core, owner in enumerate((me, 1 - me)):
            left = dense_block(held, lists[owner, 0, 0, 1 + me, k])
            partials[core, part, :] = times(left, shared_block(blocks, other, 1 + me, core, k)).astype(BF16)


def asked_blocks(far, held, picked):
    me = lax.axis_index("core")
    for k in range(SLOTS):
        for core, owner in enumerate((me, 1 - me)):
            picked[core, NV * k : NV * (k + 1), :] = dense_block(held, far[owner, 0, 1, 1 + me, k])


def third_blocks(lists, held, blocks, other, third):
    me = lax.axis_index("core")

    @pl.when(me == 0)
    def _():
        for k in range(SLOTS):
            for core in range(2):
                third[core, NV * k : NV * (k + 1), :] = dense_block(held, lists[core, 1, 1, 3, k])

    @pl.when(me == 1)
    def _():
        for k in range(SLOTS):
            for core in range(2):
                left = dense_block(held, lists[1 - core, 0, 0, 3, k])
                product = times(left, shared_block(blocks, other, 3, core, k))
                third[1 - core, NV * k : NV * (k + 1), :] = product.astype(BF16)


def early_sums(lists, far, held, blocks, back, total):
    me = lax.axis_index("core")
    total[...] = jnp.zeros_like(total)
    for k in range(SLOTS):
        part = slice(NV * k, NV * (k + 1))
        row, col = lists[me, 0, 0, 0, k], lists[me, 0, 1, 0, k]
        total[row] += times_transposed(dense_block(held, col), blocks[k])
        total[col] += times(dense_block(held, row), blocks[k])
        for core, owner in enumerate((me, 1 - me)):
            total[far[owner, 0, 1, 1 + me, k]] += back[core, part, :].astype(F32)


def packed_rows(total, *outs):
    for row in range(NBB):
        whole = total[row]
        for q in range(4):
            part = whole[:, 64 * q : 64 * q + 64]
            start = (row * 2 + q // 2) * CHUNK
            out = outs[q % 2]
            out[start : start + CHUNK, :] = jnp.concatenate([part[:32], part[32:]], axis=1).astype(out.dtype)


def late_sums(lists, early, blocks, other, right, third, kept, given, total):
    me = lax.axis_index("core")
    for k in range(SLOTS):
        part = slice(NV * k, NV * (k + 1))
        for core, owner in enumerate((me, 1 - me)):
            block = shared_block(blocks, other, 1 + me, core, k)
            total[lists[owner, 0, 0, 1 + me, k]] += times_transposed(right[core, part, :], block)

    @pl.when(me == 0)
    def _():
        for k in range(SLOTS):
            for core in range(2):
                came = third[core, NV * k : NV * (k + 1), :]
                block = shared_block(blocks, other, 3, core, k)
                total[lists[core, 0, 0, 3, k]] += times_transposed(came, block)

    @pl.when(me == 1)
    def _():
        for k in range(SLOTS):
            for core in range(2):
                total[lists[core, 1, 1, 3, k]] += third[core, NV * k : NV * (k + 1), :].astype(F32)

    @pl.when(me == 0)
    def _():
        packed_rows(total, kept, given)

    @pl.when(me == 1)
    def _():
        packed_rows(total, given, kept)


def both_cores(kept, got, out):
    theirs = got[1 - lax.axis_index("core")]
    out[...] = (kept[...] + theirs.astype(F32)).astype(BF16)


def gathered_sum(arrived, out):
    sums = [arrived[i * CHUNK : (i + 1) * CHUNK, :].astype(F32) for i in range(4)]
    for i in range(4, COL // 2):
        sums[i % 4] += arrived[i * CHUNK : (i + 1) * CHUNK, :].astype(F32)
    packed = (sums[0] + sums[1]) + (sums[2] + sums[3])
    own = jnp.concatenate([packed[:, :64], packed[:, 64:]], axis=0)
    out[...] = jnp.transpose(jnp.concatenate([own, own], axis=1))[:64]


VM = pl.BlockSpec(memory_space=pltpu.VMEM)
SM = pl.BlockSpec(memory_space=pltpu.SMEM)
PARAMS = pltpu.CompilerParams(vmem_limit_bytes=24 * 1024 * 1024)


def shape_of(shape, dtype):
    return jax.ShapeDtypeStruct(shape, dtype)


def per_device(vectors, blocks, row_blocks, col_blocks):
    stored = blocks.reshape(STEPS * SLOTS, BS, BS)
    listed = jnp.stack([row_blocks[0, 0], col_blocks[0, 0]])
    three_on = routed(listed, -3, -3)
    mine = pl.pallas_call(
        prepared,
        out_shape=shape_of((COL // 2 * CHUNK, HALF), BF16),
        in_specs=[VM],
        out_specs=VM,
        compiler_params=PARAMS,
    )(vectors)
    arriving = exchanged(lax.optimization_barrier((mine, three_on))[0], CHUNK, "pos")
    lists = lax.all_gather(jnp.stack([listed, three_on]), "core")
    far = routed(lists, -1, -2)
    other = lax.ppermute(stored, "core", [(0, 1), (1, 0)])
    held = lax.all_gather(arriving, "core", tiled=True)
    two = shape_of((2, SLOTS * NV, BS), BF16)
    partials = pl.pallas_call(
        transposed_products,
        out_shape=two,
        in_specs=[SM] + [VM] * 3,
        out_specs=VM,
        compiler_params=PARAMS,
    )(lists, held, stored, other)
    back = routed(partials, -1, -2)
    later_far, _ = lax.optimization_barrier((far, partials))
    picked = pl.pallas_call(
        asked_blocks,
        out_shape=two,
        in_specs=[SM, VM],
        out_specs=VM,
        compiler_params=PARAMS,
    )(later_far, held)
    right = routed(picked, 1, 2)
    third = pl.pallas_call(
        third_blocks,
        out_shape=two,
        in_specs=[SM] + [VM] * 3,
        out_specs=VM,
        compiler_params=PARAMS,
    )(lists, held, stored, other)
    third_sent = third
    third = routed(third, 3, -3)
    early = pl.pallas_call(
        early_sums,
        out_shape=shape_of((NBB, NV, BS), F32),
        in_specs=[SM] * 2 + [VM] * 3,
        out_specs=VM,
        compiler_params=PARAMS,
    )(lists, far, lax.optimization_barrier((held, third_sent))[0], stored, back)
    half = (COL // 2 * CHUNK, HALF)
    kept, given, _ = pl.pallas_call(
        late_sums,
        out_shape=(shape_of(half, F32), shape_of(half, BF16), shape_of((NBB, NV, BS), F32)),
        in_specs=[SM] + [VM] * 5,
        out_specs=(VM,) * 3,
        input_output_aliases={1: 2},
        compiler_params=PARAMS,
    )(lists, early, stored, other, right, third)
    chips = pl.pallas_call(
        both_cores,
        out_shape=shape_of(half, BF16),
        in_specs=[VM, VM],
        out_specs=VM,
        compiler_params=PARAMS,
    )(kept, lax.all_gather(given, "core"))
    return pl.pallas_call(
        gathered_sum,
        out_shape=shape_of((64, NV), F32),
        in_specs=[VM],
        out_specs=VM,
        compiler_params=PARAMS,
    )(exchanged(chips, CHUNK, "pos"))


def solution(mesh):
    shards, places = mesh.devices.shape
    fine = Mesh(mesh.devices.reshape(shards, places // 2, 2), AXES)
    rest = ("pos", "core")
    return jax.shard_map(
        per_device,
        mesh=fine,
        in_specs=(
            P(AXES, None),
            P("blk", rest, None, None, None, None),
            P("blk", rest, None, None),
            P("blk", rest, None, None),
        ),
        out_specs=P(AXES, None),
        check_vma=False,
    )
```

```python
import jax
import jax.numpy as jnp
from jax import lax
from jax.experimental import pallas as pl
from jax.experimental.pallas import tpu as pltpu
from jax.sharding import Mesh, PartitionSpec as P

BF16 = jnp.bfloat16
F32 = jnp.float32
COL = 64
NBB = 16
NV = 64
BS = 256
STEPS = 4
AXES = ("blk", "pos", "core")
SLOTS = 2
HALF = 128
CHUNK = 32


def routed(block, near, far):
    sizes = [lax.axis_size(axis) for axis in AXES]
    n, positions, cores = sizes
    route = []
    for shard in range(n):
        for place in range(positions * cores):
            step = far if place % cores else near
            route.append((shard * positions * cores + place, (shard + step) % n * positions * cores + place))
    return lax.ppermute(block, AXES, route)


def exchanged(flat, rows, axes):
    pieces = lax.all_to_all(flat.reshape(-1, rows, HALF), axes, 0, 0, tiled=True)
    return pieces.reshape(-1, HALF)


def dense_block(held, index):
    tops, bottoms = [], []
    for quarter in range(4):
        place = (quarter % 2) * (COL // 2) + index * 2 + quarter // 2
        start = pl.multiple_of(place * CHUNK, CHUNK)
        piece = held[pl.ds(start, CHUNK), :]
        tops.append(piece[:, :64])
        bottoms.append(piece[:, 64:])
    top = jnp.concatenate(tops, axis=1)
    bottom = jnp.concatenate(bottoms, axis=1)
    return jnp.concatenate([top, bottom], axis=0)


def times(left, block):
    return lax.dot_general(left, block, (((1,), (0,)), ((), ())), preferred_element_type=F32)


def times_transposed(left, block):
    return lax.dot_general(left, block, (((1,), (1,)), ((), ())), preferred_element_type=F32)


def prepared(vectors, out):
    rows = vectors[...]
    turned = jnp.transpose(jnp.concatenate([rows, rows], axis=1))
    packed = jnp.concatenate([turned[:32], turned[32:64]], axis=1).astype(BF16)
    for i in range(COL // 2):
        out[i * CHUNK : (i + 1) * CHUNK, :] = packed


def shared_block(blocks, other, step, core, k):
    return (other if core else blocks)[step * SLOTS + k]


def transposed_products(lists, held, blocks, other, partials):
    me = lax.axis_index("core")
    for k in range(SLOTS):
        part = slice(NV * k, NV * (k + 1))
        for core, owner in enumerate((me, 1 - me)):
            left = dense_block(held, lists[owner, 0, 1 + me, k])
            partials[core, part, :] = times(left, shared_block(blocks, other, 1 + me, core, k)).astype(BF16)


def asked_blocks(far, held, picked):
    me = lax.axis_index("core")
    for k in range(SLOTS):
        for core, owner in enumerate((me, 1 - me)):
            picked[core, NV * k : NV * (k + 1), :] = dense_block(held, far[owner, 1, 1 + me, k])


def third_blocks(lists, far3, held, blocks, other, third):
    me = lax.axis_index("core")

    @pl.when(me == 0)
    def _():
        for k in range(SLOTS):
            for core in range(2):
                third[core, NV * k : NV * (k + 1), :] = dense_block(held, far3[core, 1, 3, k])

    @pl.when(me == 1)
    def _():
        for k in range(SLOTS):
            for core in range(2):
                left = dense_block(held, lists[1 - core, 0, 3, k])
                product = times(left, shared_block(blocks, other, 3, core, k))
                third[1 - core, NV * k : NV * (k + 1), :] = product.astype(BF16)


def early_sums(lists, far, held, blocks, back, total):
    me = lax.axis_index("core")
    total[...] = jnp.zeros_like(total)
    for k in range(SLOTS):
        part = slice(NV * k, NV * (k + 1))
        row, col = lists[me, 0, 0, k], lists[me, 1, 0, k]
        total[row] += times_transposed(dense_block(held, col), blocks[k])
        total[col] += times(dense_block(held, row), blocks[k])
        for core, owner in enumerate((me, 1 - me)):
            total[far[owner, 1, 1 + me, k]] += back[core, part, :].astype(F32)


def packed_rows(total, *outs):
    first = lax.broadcasted_iota(jnp.int32, (CHUNK, HALF), 1) < 64
    for row in range(NBB):
        for half in range(2):
            whole = total[row, :, half * HALF : (half + 1) * HALF]
            top, bottom = whole[:CHUNK], whole[CHUNK:]
            pieces = (
                jnp.where(first, top, pltpu.roll(bottom, 64, 1)),
                jnp.where(first, pltpu.roll(top, 64, 1), bottom),
            )
            start = (row * 2 + half) * CHUNK
            for out, piece in zip(outs, pieces):
                out[start : start + CHUNK, :] = piece.astype(out.dtype)


def late_sums(lists, far3, early, blocks, other, right, third, kept, given, total):
    me = lax.axis_index("core")
    for k in range(SLOTS):
        part = slice(NV * k, NV * (k + 1))
        for core, owner in enumerate((me, 1 - me)):
            block = shared_block(blocks, other, 1 + me, core, k)
            total[lists[owner, 0, 1 + me, k]] += times_transposed(right[core, part, :], block)

    @pl.when(me == 0)
    def _():
        for k in range(SLOTS):
            for core in range(2):
                came = third[core, NV * k : NV * (k + 1), :]
                block = shared_block(blocks, other, 3, core, k)
                total[lists[core, 0, 3, k]] += times_transposed(came, block)

    @pl.when(me == 1)
    def _():
        for k in range(SLOTS):
            for core in range(2):
                total[far3[core, 1, 3, k]] += third[core, NV * k : NV * (k + 1), :].astype(F32)

    @pl.when(me == 0)
    def _():
        packed_rows(total, kept, given)

    @pl.when(me == 1)
    def _():
        packed_rows(total, given, kept)


def both_cores(kept, got, out):
    theirs = got[1 - lax.axis_index("core")]
    out[...] = (kept[...] + theirs.astype(F32)).astype(BF16)


def gathered_sum(arrived, out):
    sums = [arrived[i * CHUNK : (i + 1) * CHUNK, :].astype(F32) for i in range(4)]
    for i in range(4, COL // 2):
        sums[i % 4] += arrived[i * CHUNK : (i + 1) * CHUNK, :].astype(F32)
    packed = (sums[0] + sums[1]) + (sums[2] + sums[3])
    own = jnp.concatenate([packed[:, :64], packed[:, 64:]], axis=0)
    out[...] = jnp.transpose(jnp.concatenate([own, own], axis=1))[:64]


VM = pl.BlockSpec(memory_space=pltpu.VMEM)
SM = pl.BlockSpec(memory_space=pltpu.SMEM)
PARAMS = pltpu.CompilerParams(vmem_limit_bytes=24 * 1024 * 1024)


def shape_of(shape, dtype):
    return jax.ShapeDtypeStruct(shape, dtype)


def per_device(vectors, blocks, row_blocks, col_blocks):
    stored = blocks.reshape(STEPS * SLOTS, BS, BS)
    mine = pl.pallas_call(
        prepared,
        out_shape=shape_of((COL // 2 * CHUNK, HALF), BF16),
        in_specs=[VM],
        out_specs=VM,
        compiler_params=PARAMS,
    )(vectors)
    arriving = exchanged(mine, CHUNK, "pos")
    lists = lax.all_gather(jnp.stack([row_blocks[0, 0], col_blocks[0, 0]]), "core")
    far = routed(lists, -1, -2)
    other = lax.ppermute(stored, "core", [(0, 1), (1, 0)])
    held = lax.all_gather(arriving, "core", tiled=True)
    two = shape_of((2, SLOTS * NV, BS), BF16)
    partials = pl.pallas_call(
        transposed_products,
        out_shape=two,
        in_specs=[SM] + [VM] * 3,
        out_specs=VM,
        compiler_params=PARAMS,
    )(lists, held, stored, other)
    back = routed(partials, -1, -2)
    later_far, _ = lax.optimization_barrier((far, partials))
    far3 = routed(lists, -3, -3)
    picked = pl.pallas_call(
        asked_blocks,
        out_shape=two,
        in_specs=[SM, VM],
        out_specs=VM,
        compiler_params=PARAMS,
    )(later_far, held)
    right = routed(picked, 1, 2)
    third = pl.pallas_call(
        third_blocks,
        out_shape=two,
        in_specs=[SM, SM] + [VM] * 3,
        out_specs=VM,
        compiler_params=PARAMS,
    )(lists, far3, held, stored, other)
    third_sent = third
    third = routed(third, 3, -3)
    early = pl.pallas_call(
        early_sums,
        out_shape=shape_of((NBB, NV, BS), F32),
        in_specs=[SM] * 2 + [VM] * 3,
        out_specs=VM,
        compiler_params=PARAMS,
    )(lists, far, lax.optimization_barrier((held, third_sent))[0], stored, back)
    half = (COL // 2 * CHUNK, HALF)
    kept, given, _ = pl.pallas_call(
        late_sums,
        out_shape=(shape_of(half, F32), shape_of(half, BF16), shape_of((NBB, NV, BS), F32)),
        in_specs=[SM] * 2 + [VM] * 5,
        out_specs=(VM,) * 3,
        input_output_aliases={2: 2},
        compiler_params=PARAMS,
    )(lists, far3, early, stored, other, right, third)
    chips = pl.pallas_call(
        both_cores,
        out_shape=shape_of(half, BF16),
        in_specs=[VM, VM],
        out_specs=VM,
        compiler_params=PARAMS,
    )(kept, lax.all_gather(given, "core"))
    return pl.pallas_call(
        gathered_sum,
        out_shape=shape_of((64, NV), F32),
        in_specs=[VM],
        out_specs=VM,
        compiler_params=PARAMS,
    )(exchanged(chips, CHUNK, "pos"))


def solution(mesh):
    shards, places = mesh.devices.shape
    fine = Mesh(mesh.devices.reshape(shards, places // 2, 2), AXES)
    rest = ("pos", "core")
    return jax.shard_map(
        per_device,
        mesh=fine,
        in_specs=(
            P(AXES, None),
            P("blk", rest, None, None, None, None),
            P("blk", rest, None, None),
            P("blk", rest, None, None),
        ),
        out_specs=P(AXES, None),
        check_vma=False,
    )
```

```python
import jax
import jax.numpy as jnp
from jax import lax
from jax.experimental import pallas as pl
from jax.experimental.pallas import tpu as pltpu
from jax.sharding import Mesh, PartitionSpec as P

BF16 = jnp.bfloat16
F32 = jnp.float32
COL = 64
NBB = 16
NV = 64
BS = 256
STEPS = 4
AXES = ("blk", "pos", "core")
SLOTS = 2
HALF = 128
CHUNK = 32


def routed(block, near, far):
    sizes = [lax.axis_size(axis) for axis in AXES]
    n, positions, cores = sizes
    route = []
    for shard in range(n):
        for place in range(positions * cores):
            step = far if place % cores else near
            route.append((shard * positions * cores + place, (shard + step) % n * positions * cores + place))
    return lax.ppermute(block, AXES, route)


def exchanged(flat, rows, axes):
    pieces = lax.all_to_all(flat.reshape(-1, rows, HALF), axes, 0, 0, tiled=True)
    return pieces.reshape(-1, HALF)


def dense_block(held, index):
    tops, bottoms = [], []
    for quarter in range(4):
        place = (quarter % 2) * (COL // 2) + index * 2 + quarter // 2
        start = pl.multiple_of(place * CHUNK, CHUNK)
        piece = held[pl.ds(start, CHUNK), :]
        tops.append(piece[:, :64])
        bottoms.append(piece[:, 64:])
    top = jnp.concatenate(tops, axis=1)
    bottom = jnp.concatenate(bottoms, axis=1)
    return jnp.concatenate([top, bottom], axis=0)


def times(left, block):
    return lax.dot_general(left, block, (((1,), (0,)), ((), ())), preferred_element_type=F32)


def times_transposed(left, block):
    return lax.dot_general(left, block, (((1,), (1,)), ((), ())), preferred_element_type=F32)


def prepared(vectors, out):
    rows = vectors[...]
    turned = jnp.transpose(jnp.concatenate([rows, rows], axis=1))
    packed = jnp.concatenate([turned[:32], turned[32:64]], axis=1).astype(BF16)
    for i in range(COL // 2):
        out[i * CHUNK : (i + 1) * CHUNK, :] = packed


def shared_block(blocks, other, step, core, k):
    return (other if core else blocks)[step * SLOTS + k]


def transposed_products(lists, held, blocks, other, partials):
    me = lax.axis_index("core")
    for k in range(SLOTS):
        part = slice(NV * k, NV * (k + 1))
        for core, owner in enumerate((me, 1 - me)):
            left = dense_block(held, lists[owner, 0, 1 + me, k])
            partials[core, part, :] = times(left, shared_block(blocks, other, 1 + me, core, k)).astype(BF16)


def asked_blocks(far, held, picked):
    me = lax.axis_index("core")
    for k in range(SLOTS):
        for core, owner in enumerate((me, 1 - me)):
            picked[core, NV * k : NV * (k + 1), :] = dense_block(held, far[owner, 1, 1 + me, k])


def third_blocks(lists, far3, held, blocks, other, third):
    me = lax.axis_index("core")

    @pl.when(me == 0)
    def _():
        for k in range(SLOTS):
            for core in range(2):
                third[core, NV * k : NV * (k + 1), :] = dense_block(held, far3[core, 1, 3, k])

    @pl.when(me == 1)
    def _():
        for k in range(SLOTS):
            for core in range(2):
                left = dense_block(held, lists[1 - core, 0, 3, k])
                product = times(left, shared_block(blocks, other, 3, core, k))
                third[1 - core, NV * k : NV * (k + 1), :] = product.astype(BF16)


def early_sums(lists, far, held, blocks, back, total):
    me = lax.axis_index("core")
    total[...] = jnp.zeros_like(total)
    for k in range(SLOTS):
        part = slice(NV * k, NV * (k + 1))
        row, col = lists[me, 0, 0, k], lists[me, 1, 0, k]
        total[row] += times_transposed(dense_block(held, col), blocks[k])
        total[col] += times(dense_block(held, row), blocks[k])
        for core, owner in enumerate((me, 1 - me)):
            total[far[owner, 1, 1 + me, k]] += back[core, part, :].astype(F32)


def packed_rows(total, *outs):
    for row in range(NBB):
        whole = total[row]
        for q in range(4):
            part = whole[:, 64 * q : 64 * q + 64]
            start = (row * 2 + q // 2) * CHUNK
            out = outs[q % 2]
            out[start : start + CHUNK, :] = jnp.concatenate([part[:32], part[32:]], axis=1).astype(out.dtype)


def late_sums(lists, far3, early, blocks, other, right, third, kept, given, total):
    me = lax.axis_index("core")
    for k in range(SLOTS):
        part = slice(NV * k, NV * (k + 1))
        for core, owner in enumerate((me, 1 - me)):
            block = shared_block(blocks, other, 1 + me, core, k)
            total[lists[owner, 0, 1 + me, k]] += times_transposed(right[core, part, :], block)

    @pl.when(me == 0)
    def _():
        for k in range(SLOTS):
            for core in range(2):
                came = third[core, NV * k : NV * (k + 1), :]
                block = shared_block(blocks, other, 3, core, k)
                total[lists[core, 0, 3, k]] += times_transposed(came, block)

    @pl.when(me == 1)
    def _():
        for k in range(SLOTS):
            for core in range(2):
                total[far3[core, 1, 3, k]] += third[core, NV * k : NV * (k + 1), :].astype(F32)

    @pl.when(me == 0)
    def _():
        packed_rows(total, kept, given)

    @pl.when(me == 1)
    def _():
        packed_rows(total, given, kept)


def both_cores(kept, got, out):
    theirs = got[1 - lax.axis_index("core")]
    out[...] = (kept[...] + theirs.astype(F32)).astype(BF16)


def gathered_sum(arrived, out):
    sums = [arrived[i * CHUNK : (i + 1) * CHUNK, :].astype(F32) for i in range(4)]
    for i in range(4, COL // 2):
        sums[i % 4] += arrived[i * CHUNK : (i + 1) * CHUNK, :].astype(F32)
    packed = (sums[0] + sums[1]) + (sums[2] + sums[3])
    own = jnp.concatenate([packed[:, :64], packed[:, 64:]], axis=0)
    out[...] = jnp.transpose(jnp.concatenate([own, own], axis=1))[:64]


VM = pl.BlockSpec(memory_space=pltpu.VMEM)
SM = pl.BlockSpec(memory_space=pltpu.SMEM)
PARAMS = pltpu.CompilerParams(vmem_limit_bytes=24 * 1024 * 1024)


def shape_of(shape, dtype):
    return jax.ShapeDtypeStruct(shape, dtype)


def per_device(vectors, blocks, row_blocks, col_blocks):
    stored = blocks.reshape(STEPS * SLOTS, BS, BS)
    mine = pl.pallas_call(
        prepared,
        out_shape=shape_of((COL // 2 * CHUNK, HALF), BF16),
        in_specs=[VM],
        out_specs=VM,
        compiler_params=PARAMS,
    )(vectors)
    arriving = exchanged(mine, CHUNK, "pos")
    lists = lax.all_gather(jnp.stack([row_blocks[0, 0], col_blocks[0, 0]]), "core")
    far = routed(lists, -1, -2)
    other = lax.ppermute(stored, "core", [(0, 1), (1, 0)])
    held = lax.all_gather(arriving, "core", tiled=True)
    two = shape_of((2, SLOTS * NV, BS), BF16)
    partials = pl.pallas_call(
        transposed_products,
        out_shape=two,
        in_specs=[SM] + [VM] * 3,
        out_specs=VM,
        compiler_params=PARAMS,
    )(lists, held, stored, other)
    back = routed(partials, -1, -2)
    later_far, _ = lax.optimization_barrier((far, partials))
    later_lists, _ = lax.optimization_barrier((lists, partials))
    far3 = routed(later_lists, -3, -3)
    picked = pl.pallas_call(
        asked_blocks,
        out_shape=two,
        in_specs=[SM, VM],
        out_specs=VM,
        compiler_params=PARAMS,
    )(later_far, held)
    right = routed(picked, 1, 2)
    third = pl.pallas_call(
        third_blocks,
        out_shape=two,
        in_specs=[SM, SM] + [VM] * 3,
        out_specs=VM,
        compiler_params=PARAMS,
    )(lists, far3, held, stored, other)
    third = routed(third, 3, -3)
    early = pl.pallas_call(
        early_sums,
        out_shape=shape_of((NBB, NV, BS), F32),
        in_specs=[SM] * 2 + [VM] * 3,
        out_specs=VM,
        compiler_params=PARAMS,
    )(lists, far, held, stored, back)
    half = (COL // 2 * CHUNK, HALF)
    kept, given, _ = pl.pallas_call(
        late_sums,
        out_shape=(shape_of(half, F32), shape_of(half, BF16), shape_of((NBB, NV, BS), F32)),
        in_specs=[SM] * 2 + [VM] * 5,
        out_specs=(VM,) * 3,
        input_output_aliases={2: 2},
        compiler_params=PARAMS,
    )(lists, far3, early, stored, other, right, third)
    chips = pl.pallas_call(
        both_cores,
        out_shape=shape_of(half, BF16),
        in_specs=[VM, VM],
        out_specs=VM,
        compiler_params=PARAMS,
    )(kept, lax.all_gather(given, "core"))
    return pl.pallas_call(
        gathered_sum,
        out_shape=shape_of((64, NV), F32),
        in_specs=[VM],
        out_specs=VM,
        compiler_params=PARAMS,
    )(exchanged(chips, CHUNK, "pos"))


def solution(mesh):
    shards, places = mesh.devices.shape
    fine = Mesh(mesh.devices.reshape(shards, places // 2, 2), AXES)
    rest = ("pos", "core")
    return jax.shard_map(
        per_device,
        mesh=fine,
        in_specs=(
            P(AXES, None),
            P("blk", rest, None, None, None, None),
            P("blk", rest, None, None),
            P("blk", rest, None, None),
        ),
        out_specs=P(AXES, None),
        check_vma=False,
    )
```

```python
import jax
import jax.numpy as jnp
from jax import lax
from jax.experimental import pallas as pl
from jax.experimental.pallas import tpu as pltpu
from jax.sharding import Mesh, PartitionSpec as P

BF16 = jnp.bfloat16
F32 = jnp.float32
COL = 64
NBB = 16
NV = 64
BS = 256
STEPS = 4
AXES = ("blk", "pos", "core")
SLOTS = 2
HALF = 128
CHUNK = 32


def routed(block, near, far):
    sizes = [lax.axis_size(axis) for axis in AXES]
    n, positions, cores = sizes
    route = []
    for shard in range(n):
        for place in range(positions * cores):
            step = far if place % cores else near
            route.append((shard * positions * cores + place, (shard + step) % n * positions * cores + place))
    return lax.ppermute(block, AXES, route)


def exchanged(flat, rows, axes):
    pieces = lax.all_to_all(flat.reshape(-1, rows, HALF), axes, 0, 0, tiled=True)
    return pieces.reshape(-1, HALF)


def dense_block(held, index):
    tops, bottoms = [], []
    for quarter in range(4):
        place = (quarter % 2) * (COL // 2) + index * 2 + quarter // 2
        start = pl.multiple_of(place * CHUNK, CHUNK)
        piece = held[pl.ds(start, CHUNK), :]
        tops.append(piece[:, :64])
        bottoms.append(piece[:, 64:])
    top = jnp.concatenate(tops, axis=1)
    bottom = jnp.concatenate(bottoms, axis=1)
    return jnp.concatenate([top, bottom], axis=0)


def times(left, block):
    return lax.dot_general(left, block, (((1,), (0,)), ((), ())), preferred_element_type=F32)


def times_transposed(left, block):
    return lax.dot_general(left, block, (((1,), (1,)), ((), ())), preferred_element_type=F32)


def prepared(vectors, out, held_rows):
    pltpu.sync_copy(vectors, held_rows)
    rows = held_rows[...]
    turned = jnp.transpose(jnp.concatenate([rows, rows], axis=1))
    packed = jnp.concatenate([turned[:32], turned[32:64]], axis=1).astype(BF16)
    for i in range(COL // 2):
        out[i * CHUNK : (i + 1) * CHUNK, :] = packed


def shared_block(blocks, other, step, core, k):
    return (other if core else blocks)[step * SLOTS + k]


def transposed_products(lists, held, blocks, other, partials):
    me = lax.axis_index("core")
    for k in range(SLOTS):
        part = slice(NV * k, NV * (k + 1))
        for core, owner in enumerate((me, 1 - me)):
            left = dense_block(held, lists[owner, 0, 1 + me, k])
            partials[core, part, :] = times(left, shared_block(blocks, other, 1 + me, core, k)).astype(BF16)


def asked_blocks(far, held, picked):
    me = lax.axis_index("core")
    for k in range(SLOTS):
        for core, owner in enumerate((me, 1 - me)):
            picked[core, NV * k : NV * (k + 1), :] = dense_block(held, far[owner, 1, 1 + me, k])


def third_blocks(lists, far3, held, blocks, other, third):
    me = lax.axis_index("core")

    @pl.when(me == 0)
    def _():
        for k in range(SLOTS):
            for core in range(2):
                third[core, NV * k : NV * (k + 1), :] = dense_block(held, far3[core, 1, 3, k])

    @pl.when(me == 1)
    def _():
        for k in range(SLOTS):
            for core in range(2):
                left = dense_block(held, lists[1 - core, 0, 3, k])
                product = times(left, shared_block(blocks, other, 3, core, k))
                third[1 - core, NV * k : NV * (k + 1), :] = product.astype(BF16)


def early_sums(lists, far, held, blocks, back, total):
    me = lax.axis_index("core")
    total[...] = jnp.zeros_like(total)
    for k in range(SLOTS):
        part = slice(NV * k, NV * (k + 1))
        row, col = lists[me, 0, 0, k], lists[me, 1, 0, k]
        total[row] += times_transposed(dense_block(held, col), blocks[k])
        total[col] += times(dense_block(held, row), blocks[k])
        for core, owner in enumerate((me, 1 - me)):
            total[far[owner, 1, 1 + me, k]] += back[core, part, :].astype(F32)


def packed_rows(total, *outs):
    for row in range(NBB):
        whole = total[row]
        for q in range(4):
            part = whole[:, 64 * q : 64 * q + 64]
            start = (row * 2 + q // 2) * CHUNK
            out = outs[q % 2]
            out[start : start + CHUNK, :] = jnp.concatenate([part[:32], part[32:]], axis=1).astype(out.dtype)


def late_sums(lists, far3, early, blocks, other, right, third, kept, given, total):
    me = lax.axis_index("core")
    for k in range(SLOTS):
        part = slice(NV * k, NV * (k + 1))
        for core, owner in enumerate((me, 1 - me)):
            block = shared_block(blocks, other, 1 + me, core, k)
            total[lists[owner, 0, 1 + me, k]] += times_transposed(right[core, part, :], block)

    @pl.when(me == 0)
    def _():
        for k in range(SLOTS):
            for core in range(2):
                came = third[core, NV * k : NV * (k + 1), :]
                block = shared_block(blocks, other, 3, core, k)
                total[lists[core, 0, 3, k]] += times_transposed(came, block)

    @pl.when(me == 1)
    def _():
        for k in range(SLOTS):
            for core in range(2):
                total[far3[core, 1, 3, k]] += third[core, NV * k : NV * (k + 1), :].astype(F32)

    @pl.when(me == 0)
    def _():
        packed_rows(total, kept, given)

    @pl.when(me == 1)
    def _():
        packed_rows(total, given, kept)


def both_cores(kept, got, out):
    theirs = got[1 - lax.axis_index("core")]
    out[...] = (kept[...] + theirs.astype(F32)).astype(BF16)


def gathered_sum(arrived, out):
    sums = [arrived[i * CHUNK : (i + 1) * CHUNK, :].astype(F32) for i in range(4)]
    for i in range(4, COL // 2):
        sums[i % 4] += arrived[i * CHUNK : (i + 1) * CHUNK, :].astype(F32)
    packed = (sums[0] + sums[1]) + (sums[2] + sums[3])
    own = jnp.concatenate([packed[:, :64], packed[:, 64:]], axis=0)
    out[...] = jnp.transpose(jnp.concatenate([own, own], axis=1))[:64]


VM = pl.BlockSpec(memory_space=pltpu.VMEM)
SM = pl.BlockSpec(memory_space=pltpu.SMEM)
PARAMS = pltpu.CompilerParams(vmem_limit_bytes=24 * 1024 * 1024)


def shape_of(shape, dtype):
    return jax.ShapeDtypeStruct(shape, dtype)


def per_device(vectors, blocks, row_blocks, col_blocks):
    stored = blocks.reshape(STEPS * SLOTS, BS, BS)
    mine = pl.pallas_call(
        prepared,
        out_shape=shape_of((COL // 2 * CHUNK, HALF), BF16),
        in_specs=[pl.BlockSpec(memory_space=pl.ANY)],
        out_specs=VM,
        scratch_shapes=[pltpu.VMEM((64, NV), F32)],
        compiler_params=PARAMS,
    )(vectors)
    arriving = exchanged(mine, CHUNK, "pos")
    lists = lax.all_gather(jnp.stack([row_blocks[0, 0], col_blocks[0, 0]]), "core")
    far = routed(lists, -1, -2)
    other = lax.ppermute(stored, "core", [(0, 1), (1, 0)])
    held = lax.all_gather(arriving, "core", tiled=True)
    two = shape_of((2, SLOTS * NV, BS), BF16)
    partials = pl.pallas_call(
        transposed_products,
        out_shape=two,
        in_specs=[SM] + [VM] * 3,
        out_specs=VM,
        compiler_params=PARAMS,
    )(lists, held, stored, other)
    back = routed(partials, -1, -2)
    later_far, _ = lax.optimization_barrier((far, partials))
    far3 = routed(lists, -3, -3)
    picked = pl.pallas_call(
        asked_blocks,
        out_shape=two,
        in_specs=[SM, VM],
        out_specs=VM,
        compiler_params=PARAMS,
    )(later_far, held)
    right = routed(picked, 1, 2)
    third = pl.pallas_call(
        third_blocks,
        out_shape=two,
        in_specs=[SM, SM] + [VM] * 3,
        out_specs=VM,
        compiler_params=PARAMS,
    )(lists, far3, held, stored, other)
    third_sent = third
    third = routed(third, 3, -3)
    early = pl.pallas_call(
        early_sums,
        out_shape=shape_of((NBB, NV, BS), F32),
        in_specs=[SM] * 2 + [VM] * 3,
        out_specs=VM,
        compiler_params=PARAMS,
    )(lists, far, lax.optimization_barrier((held, third_sent))[0], stored, back)
    half = (COL // 2 * CHUNK, HALF)
    kept, given, _ = pl.pallas_call(
        late_sums,
        out_shape=(shape_of(half, F32), shape_of(half, BF16), shape_of((NBB, NV, BS), F32)),
        in_specs=[SM] * 2 + [VM] * 5,
        out_specs=(VM,) * 3,
        input_output_aliases={2: 2},
        compiler_params=PARAMS,
    )(lists, far3, early, stored, other, right, third)
    chips = pl.pallas_call(
        both_cores,
        out_shape=shape_of(half, BF16),
        in_specs=[VM, VM],
        out_specs=VM,
        compiler_params=PARAMS,
    )(kept, lax.all_gather(given, "core"))
    return pl.pallas_call(
        gathered_sum,
        out_shape=shape_of((64, NV), F32),
        in_specs=[VM],
        out_specs=VM,
        compiler_params=PARAMS,
    )(exchanged(chips, CHUNK, "pos"))


def solution(mesh):
    shards, places = mesh.devices.shape
    fine = Mesh(mesh.devices.reshape(shards, places // 2, 2), AXES)
    rest = ("pos", "core")
    return jax.shard_map(
        per_device,
        mesh=fine,
        in_specs=(
            P(AXES, None),
            P("blk", rest, None, None, None, None),
            P("blk", rest, None, None),
            P("blk", rest, None, None),
        ),
        out_specs=P(AXES, None),
        check_vma=False,
    )
```

```python
import jax
import jax.numpy as jnp
from jax import lax
from jax.experimental import pallas as pl
from jax.experimental.pallas import tpu as pltpu
from jax.sharding import Mesh, PartitionSpec as P

BF16 = jnp.bfloat16
F32 = jnp.float32
COL = 64
NBB = 16
NV = 64
BS = 256
STEPS = 4
AXES = ("blk", "pos", "core")
SLOTS = 2
HALF = 128
CHUNK = 32


def routed(block, near, far):
    sizes = [lax.axis_size(axis) for axis in AXES]
    n, positions, cores = sizes
    route = []
    for shard in range(n):
        for place in range(positions * cores):
            step = far if place % cores else near
            route.append((shard * positions * cores + place, (shard + step) % n * positions * cores + place))
    return lax.ppermute(block, AXES, route)


def exchanged(flat, rows, axes):
    pieces = lax.all_to_all(flat.reshape(-1, rows, HALF), axes, 0, 0, tiled=True)
    return pieces.reshape(-1, HALF)


def dense_block(held, index):
    tops, bottoms = [], []
    for quarter in range(4):
        start = pl.multiple_of((index * 4 + quarter) * CHUNK, CHUNK)
        piece = held[pl.ds(start, CHUNK), :]
        tops.append(piece[:, :64])
        bottoms.append(piece[:, 64:])
    top = jnp.concatenate(tops, axis=1)
    bottom = jnp.concatenate(bottoms, axis=1)
    return jnp.concatenate([top, bottom], axis=0)


def times(left, block):
    return lax.dot_general(left, block, (((1,), (0,)), ((), ())), preferred_element_type=F32)


def times_transposed(left, block):
    return lax.dot_general(left, block, (((1,), (1,)), ((), ())), preferred_element_type=F32)


def prepared(vectors, out):
    rows = vectors[...]
    turned = jnp.transpose(jnp.concatenate([rows, rows], axis=1))
    packed = jnp.concatenate([turned[:32], turned[32:64]], axis=1).astype(BF16)
    for i in range(COL):
        out[i * CHUNK : (i + 1) * CHUNK, :] = packed


def shared_block(blocks, other, step, core, k):
    return (other if core else blocks)[step * SLOTS + k]


def transposed_products(lists, held, blocks, other, partials):
    me = lax.axis_index("core")
    for k in range(SLOTS):
        part = slice(NV * k, NV * (k + 1))
        for core, owner in enumerate((me, 1 - me)):
            left = dense_block(held, lists[owner, 0, 1 + me, k])
            partials[core, part, :] = times(left, shared_block(blocks, other, 1 + me, core, k)).astype(BF16)


def asked_blocks(far, held, picked):
    me = lax.axis_index("core")
    for k in range(SLOTS):
        for core, owner in enumerate((me, 1 - me)):
            picked[core, NV * k : NV * (k + 1), :] = dense_block(held, far[owner, 1, 1 + me, k])


def third_blocks(lists, far3, held, blocks, other, third):
    me = lax.axis_index("core")

    @pl.when(me == 0)
    def _():
        for k in range(SLOTS):
            for core in range(2):
                third[core, NV * k : NV * (k + 1), :] = dense_block(held, far3[core, 1, 3, k])

    @pl.when(me == 1)
    def _():
        for k in range(SLOTS):
            for core in range(2):
                left = dense_block(held, lists[1 - core, 0, 3, k])
                product = times(left, shared_block(blocks, other, 3, core, k))
                third[1 - core, NV * k : NV * (k + 1), :] = product.astype(BF16)


def early_sums(lists, far, held, blocks, back, total):
    me = lax.axis_index("core")
    total[...] = jnp.zeros_like(total)
    for k in range(SLOTS):
        part = slice(NV * k, NV * (k + 1))
        row, col = lists[me, 0, 0, k], lists[me, 1, 0, k]
        total[row] += times_transposed(dense_block(held, col), blocks[k])
        total[col] += times(dense_block(held, row), blocks[k])
        for core, owner in enumerate((me, 1 - me)):
            total[far[owner, 1, 1 + me, k]] += back[core, part, :].astype(F32)


def packed_rows(total, *outs):
    for row in range(NBB):
        whole = total[row]
        for q in range(4):
            part = whole[:, 64 * q : 64 * q + 64]
            start = (row * 2 + q // 2) * CHUNK
            out = outs[q % 2]
            out[start : start + CHUNK, :] = jnp.concatenate([part[:32], part[32:]], axis=1).astype(out.dtype)


def late_sums(lists, far3, early, blocks, other, right, third, kept, given, total):
    me = lax.axis_index("core")
    for k in range(SLOTS):
        part = slice(NV * k, NV * (k + 1))
        for core, owner in enumerate((me, 1 - me)):
            block = shared_block(blocks, other, 1 + me, core, k)
            total[lists[owner, 0, 1 + me, k]] += times_transposed(right[core, part, :], block)

    @pl.when(me == 0)
    def _():
        for k in range(SLOTS):
            for core in range(2):
                came = third[core, NV * k : NV * (k + 1), :]
                block = shared_block(blocks, other, 3, core, k)
                total[lists[core, 0, 3, k]] += times_transposed(came, block)

    @pl.when(me == 1)
    def _():
        for k in range(SLOTS):
            for core in range(2):
                total[far3[core, 1, 3, k]] += third[core, NV * k : NV * (k + 1), :].astype(F32)

    @pl.when(me == 0)
    def _():
        packed_rows(total, kept, given)

    @pl.when(me == 1)
    def _():
        packed_rows(total, given, kept)


def both_cores(kept, got, out):
    theirs = got[1 - lax.axis_index("core")]
    out[...] = (kept[...] + theirs.astype(F32)).astype(BF16)


def gathered_sum(arrived, out):
    sums = [arrived[i * CHUNK : (i + 1) * CHUNK, :].astype(F32) for i in range(4)]
    for i in range(4, COL // 2):
        sums[i % 4] += arrived[i * CHUNK : (i + 1) * CHUNK, :].astype(F32)
    packed = (sums[0] + sums[1]) + (sums[2] + sums[3])
    own = jnp.concatenate([packed[:, :64], packed[:, 64:]], axis=0)
    out[...] = jnp.transpose(jnp.concatenate([own, own], axis=1))[:64]


VM = pl.BlockSpec(memory_space=pltpu.VMEM)
SM = pl.BlockSpec(memory_space=pltpu.SMEM)
PARAMS = pltpu.CompilerParams(vmem_limit_bytes=24 * 1024 * 1024)


def shape_of(shape, dtype):
    return jax.ShapeDtypeStruct(shape, dtype)


def per_device(vectors, blocks, row_blocks, col_blocks):
    stored = blocks.reshape(STEPS * SLOTS, BS, BS)
    mine = pl.pallas_call(
        prepared,
        out_shape=shape_of((COL * CHUNK, HALF), BF16),
        in_specs=[VM],
        out_specs=VM,
        compiler_params=PARAMS,
    )(vectors)
    held = exchanged(mine, CHUNK, ("pos", "core"))
    lists = lax.all_gather(jnp.stack([row_blocks[0, 0], col_blocks[0, 0]]), "core")
    far = routed(lists, -1, -2)
    other = lax.ppermute(stored, "core", [(0, 1), (1, 0)])
    two = shape_of((2, SLOTS * NV, BS), BF16)
    partials = pl.pallas_call(
        transposed_products,
        out_shape=two,
        in_specs=[SM] + [VM] * 3,
        out_specs=VM,
        compiler_params=PARAMS,
    )(lists, held, stored, other)
    back = routed(partials, -1, -2)
    later_far, _ = lax.optimization_barrier((far, partials))
    far3 = routed(lists, -3, -3)
    picked = pl.pallas_call(
        asked_blocks,
        out_shape=two,
        in_specs=[SM, VM],
        out_specs=VM,
        compiler_params=PARAMS,
    )(later_far, held)
    right = routed(picked, 1, 2)
    third = pl.pallas_call(
        third_blocks,
        out_shape=two,
        in_specs=[SM, SM] + [VM] * 3,
        out_specs=VM,
        compiler_params=PARAMS,
    )(lists, far3, held, stored, other)
    third_sent = third
    third = routed(third, 3, -3)
    early = pl.pallas_call(
        early_sums,
        out_shape=shape_of((NBB, NV, BS), F32),
        in_specs=[SM] * 2 + [VM] * 3,
        out_specs=VM,
        compiler_params=PARAMS,
    )(lists, far, lax.optimization_barrier((held, third_sent))[0], stored, back)
    half = (COL // 2 * CHUNK, HALF)
    kept, given, _ = pl.pallas_call(
        late_sums,
        out_shape=(shape_of(half, F32), shape_of(half, BF16), shape_of((NBB, NV, BS), F32)),
        in_specs=[SM] * 2 + [VM] * 5,
        out_specs=(VM,) * 3,
        input_output_aliases={2: 2},
        compiler_params=PARAMS,
    )(lists, far3, early, stored, other, right, third)
    chips = pl.pallas_call(
        both_cores,
        out_shape=shape_of(half, BF16),
        in_specs=[VM, VM],
        out_specs=VM,
        compiler_params=PARAMS,
    )(kept, lax.all_gather(given, "core"))
    return pl.pallas_call(
        gathered_sum,
        out_shape=shape_of((64, NV), F32),
        in_specs=[VM],
        out_specs=VM,
        compiler_params=PARAMS,
    )(exchanged(chips, CHUNK, "pos"))


def solution(mesh):
    shards, places = mesh.devices.shape
    fine = Mesh(mesh.devices.reshape(shards, places // 2, 2), AXES)
    rest = ("pos", "core")
    return jax.shard_map(
        per_device,
        mesh=fine,
        in_specs=(
            P(AXES, None),
            P("blk", rest, None, None, None, None),
            P("blk", rest, None, None),
            P("blk", rest, None, None),
        ),
        out_specs=P(AXES, None),
        check_vma=False,
    )
```

```python
import jax
import jax.numpy as jnp
from jax import lax
from jax.experimental import pallas as pl
from jax.experimental.pallas import tpu as pltpu
from jax.sharding import Mesh, PartitionSpec as P

BF16 = jnp.bfloat16
F32 = jnp.float32
COL = 64
NBB = 16
NV = 64
BS = 256
STEPS = 4
AXES = ("blk", "pos", "core")
SLOTS = 2
HALF = 128
CHUNK = 32


def routed(block, near, far):
    sizes = [lax.axis_size(axis) for axis in AXES]
    n, positions, cores = sizes
    route = []
    for shard in range(n):
        for place in range(positions * cores):
            step = far if place % cores else near
            route.append((shard * positions * cores + place, (shard + step) % n * positions * cores + place))
    return lax.ppermute(block, AXES, route)


def exchanged(flat, rows, axes):
    pieces = lax.all_to_all(flat.reshape(-1, rows, HALF), axes, 0, 0, tiled=True)
    return pieces.reshape(-1, HALF)


def dense_block(held, index):
    tops, bottoms = [], []
    for quarter in range(4):
        place = (quarter % 2) * (COL // 2) + index * 2 + quarter // 2
        start = pl.multiple_of(place * CHUNK, CHUNK)
        piece = held[pl.ds(start, CHUNK), :]
        tops.append(piece[:, :64])
        bottoms.append(piece[:, 64:])
    top = jnp.concatenate(tops, axis=1)
    bottom = jnp.concatenate(bottoms, axis=1)
    return jnp.concatenate([top, bottom], axis=0)


def times(left, block):
    return lax.dot_general(left, block, (((1,), (0,)), ((), ())), preferred_element_type=F32)


def times_transposed(left, block):
    return lax.dot_general(left, block, (((1,), (1,)), ((), ())), preferred_element_type=F32)


def prepared(vectors, out):
    rows = vectors[...]
    turned = jnp.transpose(jnp.concatenate([rows, rows], axis=1))
    packed = jnp.concatenate([turned[:32], turned[32:64]], axis=1).astype(BF16)
    for i in range(COL // 2):
        out[i * CHUNK : (i + 1) * CHUNK, :] = packed


def shared_block(blocks, other, step, core, k):
    return other[(step - 1) * SLOTS + k] if core else blocks[step * SLOTS + k]


def transposed_products(lists, held, blocks, other, partials):
    me = lax.axis_index("core")
    for k in range(SLOTS):
        part = slice(NV * k, NV * (k + 1))
        for core, owner in enumerate((me, 1 - me)):
            left = dense_block(held, lists[owner, 0, 1 + me, k])
            partials[core, part, :] = times(left, shared_block(blocks, other, 1 + me, core, k)).astype(BF16)


def asked_blocks(far, held, picked):
    me = lax.axis_index("core")
    for k in range(SLOTS):
        for core, owner in enumerate((me, 1 - me)):
            picked[core, NV * k : NV * (k + 1), :] = dense_block(held, far[owner, 1, 1 + me, k])


def third_blocks(lists, far3, held, blocks, other, third):
    me = lax.axis_index("core")

    @pl.when(me == 0)
    def _():
        for k in range(SLOTS):
            for core in range(2):
                third[core, NV * k : NV * (k + 1), :] = dense_block(held, far3[core, 1, 3, k])

    @pl.when(me == 1)
    def _():
        for k in range(SLOTS):
            for core in range(2):
                left = dense_block(held, lists[1 - core, 0, 3, k])
                product = times(left, shared_block(blocks, other, 3, core, k))
                third[1 - core, NV * k : NV * (k + 1), :] = product.astype(BF16)


def early_sums(lists, far, held, blocks, back, total):
    me = lax.axis_index("core")
    total[...] = jnp.zeros_like(total)
    for k in range(SLOTS):
        part = slice(NV * k, NV * (k + 1))
        row, col = lists[me, 0, 0, k], lists[me, 1, 0, k]
        total[row] += times_transposed(dense_block(held, col), blocks[k])
        total[col] += times(dense_block(held, row), blocks[k])
        for core, owner in enumerate((me, 1 - me)):
            total[far[owner, 1, 1 + me, k]] += back[core, part, :].astype(F32)


def packed_rows(total, *outs):
    for row in range(NBB):
        whole = total[row]
        for q in range(4):
            part = whole[:, 64 * q : 64 * q + 64]
            start = (row * 2 + q // 2) * CHUNK
            out = outs[q % 2]
            out[start : start + CHUNK, :] = jnp.concatenate([part[:32], part[32:]], axis=1).astype(out.dtype)


def late_sums(lists, far3, early, blocks, other, right, third, kept, given, total):
    me = lax.axis_index("core")
    for k in range(SLOTS):
        part = slice(NV * k, NV * (k + 1))
        for core, owner in enumerate((me, 1 - me)):
            block = shared_block(blocks, other, 1 + me, core, k)
            total[lists[owner, 0, 1 + me, k]] += times_transposed(right[core, part, :], block)

    @pl.when(me == 0)
    def _():
        for k in range(SLOTS):
            for core in range(2):
                came = third[core, NV * k : NV * (k + 1), :]
                block = shared_block(blocks, other, 3, core, k)
                total[lists[core, 0, 3, k]] += times_transposed(came, block)

    @pl.when(me == 1)
    def _():
        for k in range(SLOTS):
            for core in range(2):
                total[far3[core, 1, 3, k]] += third[core, NV * k : NV * (k + 1), :].astype(F32)

    @pl.when(me == 0)
    def _():
        packed_rows(total, kept, given)

    @pl.when(me == 1)
    def _():
        packed_rows(total, given, kept)


def both_cores(kept, got, out):
    theirs = got[1 - lax.axis_index("core")]
    out[...] = (kept[...] + theirs.astype(F32)).astype(BF16)


def gathered_sum(arrived, out):
    sums = [arrived[i * CHUNK : (i + 1) * CHUNK, :].astype(F32) for i in range(4)]
    for i in range(4, COL // 2):
        sums[i % 4] += arrived[i * CHUNK : (i + 1) * CHUNK, :].astype(F32)
    packed = (sums[0] + sums[1]) + (sums[2] + sums[3])
    own = jnp.concatenate([packed[:, :64], packed[:, 64:]], axis=0)
    out[...] = jnp.transpose(jnp.concatenate([own, own], axis=1))[:64]


VM = pl.BlockSpec(memory_space=pltpu.VMEM)
SM = pl.BlockSpec(memory_space=pltpu.SMEM)
PARAMS = pltpu.CompilerParams(vmem_limit_bytes=24 * 1024 * 1024)


def shape_of(shape, dtype):
    return jax.ShapeDtypeStruct(shape, dtype)


def per_device(vectors, blocks, row_blocks, col_blocks):
    stored = blocks.reshape(STEPS * SLOTS, BS, BS)
    mine = pl.pallas_call(
        prepared,
        out_shape=shape_of((COL // 2 * CHUNK, HALF), BF16),
        in_specs=[VM],
        out_specs=VM,
        compiler_params=PARAMS,
    )(vectors)
    arriving = exchanged(mine, CHUNK, "pos")
    lists = lax.all_gather(jnp.stack([row_blocks[0, 0], col_blocks[0, 0]]), "core")
    far = routed(lists, -1, -2)
    later, _ = lax.optimization_barrier((stored[SLOTS:], lists))
    other = lax.ppermute(later, "core", [(0, 1), (1, 0)])
    held = lax.all_gather(arriving, "core", tiled=True)
    two = shape_of((2, SLOTS * NV, BS), BF16)
    partials = pl.pallas_call(
        transposed_products,
        out_shape=two,
        in_specs=[SM] + [VM] * 3,
        out_specs=VM,
        compiler_params=PARAMS,
    )(lists, held, stored, other)
    back = routed(partials, -1, -2)
    later_far, _ = lax.optimization_barrier((far, partials))
    far3 = routed(lists, -3, -3)
    picked = pl.pallas_call(
        asked_blocks,
        out_shape=two,
        in_specs=[SM, VM],
        out_specs=VM,
        compiler_params=PARAMS,
    )(later_far, held)
    right = routed(picked, 1, 2)
    third = pl.pallas_call(
        third_blocks,
        out_shape=two,
        in_specs=[SM, SM] + [VM] * 3,
        out_specs=VM,
        compiler_params=PARAMS,
    )(lists, far3, held, stored, other)
    third_sent = third
    third = routed(third, 3, -3)
    early = pl.pallas_call(
        early_sums,
        out_shape=shape_of((NBB, NV, BS), F32),
        in_specs=[SM] * 2 + [VM] * 3,
        out_specs=VM,
        compiler_params=PARAMS,
    )(lists, far, lax.optimization_barrier((held, third_sent))[0], stored, back)
    half = (COL // 2 * CHUNK, HALF)
    kept, given, _ = pl.pallas_call(
        late_sums,
        out_shape=(shape_of(half, F32), shape_of(half, BF16), shape_of((NBB, NV, BS), F32)),
        in_specs=[SM] * 2 + [VM] * 5,
        out_specs=(VM,) * 3,
        input_output_aliases={2: 2},
        compiler_params=PARAMS,
    )(lists, far3, early, stored, other, right, third)
    chips = pl.pallas_call(
        both_cores,
        out_shape=shape_of(half, BF16),
        in_specs=[VM, VM],
        out_specs=VM,
        compiler_params=PARAMS,
    )(kept, lax.all_gather(given, "core"))
    return pl.pallas_call(
        gathered_sum,
        out_shape=shape_of((64, NV), F32),
        in_specs=[VM],
        out_specs=VM,
        compiler_params=PARAMS,
    )(exchanged(chips, CHUNK, "pos"))


def solution(mesh):
    shards, places = mesh.devices.shape
    fine = Mesh(mesh.devices.reshape(shards, places // 2, 2), AXES)
    rest = ("pos", "core")
    return jax.shard_map(
        per_device,
        mesh=fine,
        in_specs=(
            P(AXES, None),
            P("blk", rest, None, None, None, None),
            P("blk", rest, None, None),
            P("blk", rest, None, None),
        ),
        out_specs=P(AXES, None),
        check_vma=False,
    )
```

```python
import jax
import jax.numpy as jnp
from jax import lax
from jax.experimental import pallas as pl
from jax.experimental.pallas import tpu as pltpu
from jax.sharding import Mesh, PartitionSpec as P

BF16 = jnp.bfloat16
F32 = jnp.float32
COL = 64
NBB = 16
NV = 64
BS = 256
STEPS = 4
AXES = ("blk", "pos", "core")
SLOTS = 2
HALF = 128
CHUNK = 32


def routed(block, near, far):
    sizes = [lax.axis_size(axis) for axis in AXES]
    n, positions, cores = sizes
    route = []
    for shard in range(n):
        for place in range(positions * cores):
            step = far if place % cores else near
            route.append((shard * positions * cores + place, (shard + step) % n * positions * cores + place))
    return lax.ppermute(block, AXES, route)


def exchanged(flat, rows, axes):
    pieces = lax.all_to_all(flat.reshape(-1, rows, HALF), axes, 0, 0, tiled=True)
    return pieces.reshape(-1, HALF)


def dense_block(held, index):
    tops, bottoms = [], []
    for quarter in range(4):
        place = (quarter % 2) * (COL // 2) + index * 2 + quarter // 2
        start = pl.multiple_of(place * CHUNK, CHUNK)
        piece = held[pl.ds(start, CHUNK), :]
        tops.append(piece[:, :64])
        bottoms.append(piece[:, 64:])
    top = jnp.concatenate(tops, axis=1)
    bottom = jnp.concatenate(bottoms, axis=1)
    return jnp.concatenate([top, bottom], axis=0)


def times(left, block):
    return lax.dot_general(left, block, (((1,), (0,)), ((), ())), preferred_element_type=F32)


def times_transposed(left, block):
    return lax.dot_general(left, block, (((1,), (1,)), ((), ())), preferred_element_type=F32)


def prepared(vectors, out):
    rows = vectors[...]
    turned = jnp.transpose(jnp.concatenate([rows, rows], axis=1))
    packed = jnp.concatenate([turned[:32], turned[32:64]], axis=1).astype(BF16)
    for i in range(COL // 2):
        out[i * CHUNK : (i + 1) * CHUNK, :] = packed


def shared_block(blocks, other, step, core, k):
    return (other if core else blocks)[step * SLOTS + k]


def transposed_products(lists, held, blocks, other, partials):
    me = lax.axis_index("core")
    for k in range(SLOTS):
        part = slice(NV * k, NV * (k + 1))
        for core, owner in enumerate((me, 1 - me)):
            left = dense_block(held, lists[owner, 0, 1 + me, k])
            partials[core, part, :] = times(left, shared_block(blocks, other, 1 + me, core, k)).astype(BF16)


def asked_blocks(far, held, picked):
    me = lax.axis_index("core")
    for k in range(SLOTS):
        for core, owner in enumerate((me, 1 - me)):
            picked[core, NV * k : NV * (k + 1), :] = dense_block(held, far[owner, 1, 1 + me, k])


def third_blocks(lists, far3, held, blocks, other, third):
    me = lax.axis_index("core")

    @pl.when(me == 0)
    def _():
        for k in range(SLOTS):
            for core in range(2):
                third[core, NV * k : NV * (k + 1), :] = dense_block(held, far3[core, 1, 3, k])

    @pl.when(me == 1)
    def _():
        for k in range(SLOTS):
            for core in range(2):
                left = dense_block(held, lists[1 - core, 0, 3, k])
                product = times(left, shared_block(blocks, other, 3, core, k))
                third[1 - core, NV * k : NV * (k + 1), :] = product.astype(BF16)


def early_sums(lists, far, held, blocks, back, total):
    me = lax.axis_index("core")
    total[...] = jnp.zeros_like(total)
    for k in range(SLOTS):
        part = slice(NV * k, NV * (k + 1))
        row, col = lists[me, 0, 0, k], lists[me, 1, 0, k]
        total[row] += times_transposed(dense_block(held, col), blocks[k])
        total[col] += times(dense_block(held, row), blocks[k])
        for core, owner in enumerate((me, 1 - me)):
            total[far[owner, 1, 1 + me, k]] += back[core, part, :].astype(F32)


def packed_rows(total, *outs):
    for row in range(NBB):
        whole = total[row]
        for q in range(4):
            part = whole[:, 64 * q : 64 * q + 64]
            start = (row * 2 + q // 2) * CHUNK
            out = outs[q % 2]
            out[start : start + CHUNK, :] = jnp.concatenate([part[:32], part[32:]], axis=1).astype(out.dtype)


def late_sums(lists, far3, early, blocks, other, right, third, kept, given, total):
    me = lax.axis_index("core")
    for k in range(SLOTS):
        part = slice(NV * k, NV * (k + 1))
        for core, owner in enumerate((me, 1 - me)):
            block = shared_block(blocks, other, 1 + me, core, k)
            total[lists[owner, 0, 1 + me, k]] += times_transposed(right[core, part, :], block)

    @pl.when(me == 0)
    def _():
        for k in range(SLOTS):
            for core in range(2):
                came = third[core, NV * k : NV * (k + 1), :]
                block = shared_block(blocks, other, 3, core, k)
                total[lists[core, 0, 3, k]] += times_transposed(came, block)

    @pl.when(me == 1)
    def _():
        for k in range(SLOTS):
            for core in range(2):
                total[far3[core, 1, 3, k]] += third[core, NV * k : NV * (k + 1), :].astype(F32)

    @pl.when(me == 0)
    def _():
        packed_rows(total, kept, given)

    @pl.when(me == 1)
    def _():
        packed_rows(total, given, kept)


def both_cores(kept, got, out):
    theirs = got[1 - lax.axis_index("core")]
    out[...] = (kept[...] + theirs.astype(F32)).astype(BF16)


def gathered_sum(arrived, out):
    sums = [arrived[i * CHUNK : (i + 1) * CHUNK, :].astype(F32) for i in range(4)]
    for i in range(4, COL // 2):
        sums[i % 4] += arrived[i * CHUNK : (i + 1) * CHUNK, :].astype(F32)
    packed = (sums[0] + sums[1]) + (sums[2] + sums[3])
    own = jnp.concatenate([packed[:, :64], packed[:, 64:]], axis=0)
    out[...] = jnp.transpose(jnp.concatenate([own, own], axis=1))[:64]


VM = pl.BlockSpec(memory_space=pltpu.VMEM)
SM = pl.BlockSpec(memory_space=pltpu.SMEM)
PARAMS = pltpu.CompilerParams(vmem_limit_bytes=24 * 1024 * 1024)


def shape_of(shape, dtype):
    return jax.ShapeDtypeStruct(shape, dtype)


def per_device(vectors, blocks, row_blocks, col_blocks):
    stored = blocks.reshape(STEPS * SLOTS, BS, BS)
    listed = jnp.stack([row_blocks[0, 0], col_blocks[0, 0]])
    mine = pl.pallas_call(
        prepared,
        out_shape=shape_of((COL // 2 * CHUNK, HALF), BF16),
        in_specs=[VM],
        out_specs=VM,
        compiler_params=PARAMS,
    )(vectors)
    arriving = exchanged(lax.optimization_barrier((mine, listed))[0], CHUNK, "pos")
    lists = lax.all_gather(listed, "core")
    far = routed(lists, -1, -2)
    whole, _ = lax.optimization_barrier((stored, listed))
    other = lax.ppermute(whole, "core", [(0, 1), (1, 0)])
    held = lax.all_gather(arriving, "core", tiled=True)
    two = shape_of((2, SLOTS * NV, BS), BF16)
    partials = pl.pallas_call(
        transposed_products,
        out_shape=two,
        in_specs=[SM] + [VM] * 3,
        out_specs=VM,
        compiler_params=PARAMS,
    )(lists, held, stored, other)
    back = routed(partials, -1, -2)
    later_far, _ = lax.optimization_barrier((far, partials))
    far3 = routed(lists, -3, -3)
    picked = pl.pallas_call(
        asked_blocks,
        out_shape=two,
        in_specs=[SM, VM],
        out_specs=VM,
        compiler_params=PARAMS,
    )(later_far, held)
    right = routed(picked, 1, 2)
    third = pl.pallas_call(
        third_blocks,
        out_shape=two,
        in_specs=[SM, SM] + [VM] * 3,
        out_specs=VM,
        compiler_params=PARAMS,
    )(lists, far3, held, stored, other)
    third_sent = third
    third = routed(third, 3, -3)
    early = pl.pallas_call(
        early_sums,
        out_shape=shape_of((NBB, NV, BS), F32),
        in_specs=[SM] * 2 + [VM] * 3,
        out_specs=VM,
        compiler_params=PARAMS,
    )(lists, far, lax.optimization_barrier((held, third_sent))[0], stored, back)
    half = (COL // 2 * CHUNK, HALF)
    kept, given, _ = pl.pallas_call(
        late_sums,
        out_shape=(shape_of(half, F32), shape_of(half, BF16), shape_of((NBB, NV, BS), F32)),
        in_specs=[SM] * 2 + [VM] * 5,
        out_specs=(VM,) * 3,
        input_output_aliases={2: 2},
        compiler_params=PARAMS,
    )(lists, far3, early, stored, other, right, third)
    chips = pl.pallas_call(
        both_cores,
        out_shape=shape_of(half, BF16),
        in_specs=[VM, VM],
        out_specs=VM,
        compiler_params=PARAMS,
    )(kept, lax.all_gather(given, "core"))
    return pl.pallas_call(
        gathered_sum,
        out_shape=shape_of((64, NV), F32),
        in_specs=[VM],
        out_specs=VM,
        compiler_params=PARAMS,
    )(exchanged(chips, CHUNK, "pos"))


def solution(mesh):
    shards, places = mesh.devices.shape
    fine = Mesh(mesh.devices.reshape(shards, places // 2, 2), AXES)
    rest = ("pos", "core")
    return jax.shard_map(
        per_device,
        mesh=fine,
        in_specs=(
            P(AXES, None),
            P("blk", rest, None, None, None, None),
            P("blk", rest, None, None),
            P("blk", rest, None, None),
        ),
        out_specs=P(AXES, None),
        check_vma=False,
    )
```
